32 devices in a mesh: dp: 2 (over y), shard: 16 (over z, x, core).
Axes of the slice: x: 2, y: 2, z: 4, core: 2. Of those that a mesh axis runs over, the one named last changes fastest.
Arguments:
- queries: bfloat16 [8192, 1024], P(('dp', 'shard')), may hold values from -16 to 16
- passages: bfloat16 [8192, 1024], P(('dp', 'shard')), may hold values from -5 to 5
- block_lists: int32 [32, 4], P('dp'), may hold values from 0 to 15, as said below
- inv_temp: float32 [], replicated, may hold values from 0.02 to 0.05
Outputs:
- query_grad: bfloat16 [8192, 1024], P(('dp', 'shard'))
- passage_grad: bfloat16 [8192, 1024], P(('dp', 'shard'))
- loss_mean: float32 [], replicated
- temp_grad: float32 [], replicated
The draws below stay inside these ranges and needn't reach their ends.
Inputs may be any that keep to these rules, and one draw needn't show every extreme that they name: `block_lists`: column 0 of row t * 16 + s names the positive passage block and columns 1 to 3 the negative passage blocks of query block t * 16 + s, as numbers within data group t; a row's numbers are distinct; the positives of one group's query blocks are a permutation of its 16 blocks.
All inputs are finite; a program needn't handle non-finite values.
Results may differ from the reference program's by a relative error of at most 0.0041.
Values may be sent and summed in bfloat16 or wider, within the bound.
A program may use at most 64 MiB of HBM per device.

```python
import math
import jax
import jax.numpy as jnp
from jax import lax

D = 1024
BLK = 256
NEG = 3
GROUP = 16
BLOCKS = 32
TOKENS = 8192


def lists_for(base_key):

    def group_lists(group_key):
        key_a, key_b, key_c = jax.random.split(group_key, 3)
        positive = jax.random.permutation(key_a, GROUP).astype(jnp.int32)
        popularity = jax.random.randint(key_b, (GROUP,), 0, 4) * GROUP
        jitter_part = jax.random.randint(key_c, (GROUP, GROUP), 0, GROUP)
        scores = popularity[None, :] + jitter_part
        columns = jnp.arange(GROUP, dtype=jnp.int32)
        scores = jnp.where(columns[None, :] == positive[:, None], -1, scores)
        distinct = scores * GROUP + columns[None, :]
        unused, picked = lax.top_k(distinct, NEG)
        return jnp.concatenate([positive[:, None], picked.astype(jnp.int32)], axis=1)
    split_keys = jax.random.split(jax.random.fold_in(base_key, 5), BLOCKS // GROUP)
    return jax.vmap(group_lists)(split_keys).reshape(BLOCKS, NEG + 1)


def passage_values(base_key, scale_low):
    key_a = jax.random.fold_in(jax.random.fold_in(base_key, 11), 0)
    key_c = jax.random.fold_in(jax.random.fold_in(base_key, 11), 2)
    normal_part = jnp.clip(jax.random.normal(key_a, (TOKENS, D), jnp.float32), -5.0, 5.0)
    log_low = jnp.log(jnp.float32(scale_low))
    row_scale = jnp.exp(jax.random.uniform(key_c, (TOKENS, 1), jnp.float32, log_low, -log_low + 1e-07))
    row_scale = jnp.minimum(row_scale, 1.0)
    return normal_part * row_scale


def draw_block_lists(key, part):
    return lists_for(key)


def draw_passages(key, part):
    values = passage_values(key, 1.0)
    return values.astype(jnp.bfloat16)


def draw_queries(key, part):
    scale_low = 1.0
    key = jax.random.fold_in(key, 23)
    own_values = passage_values(key, scale_low)
    values = own_values
    return values.astype(jnp.bfloat16)


def setup_inputs(seed: int = 0) -> dict:
    splits = jax.random.split(jax.random.key(seed), 5)
    queries = draw_queries(jax.random.fold_in(splits[4], 71), 0)
    passages = draw_passages(jax.random.fold_in(splits[4], 71), 0)
    block_lists = draw_block_lists(jax.random.fold_in(splits[4], 71), 0)
    inv_temp = jnp.clip(jnp.exp(jax.random.uniform(splits[3], (), jnp.float32, math.log(0.02), math.log(0.05))), 0.02, 0.05)
    return dict(queries=queries, passages=passages, block_lists=block_lists, inv_temp=inv_temp)


def reference(queries, passages, block_lists, inv_temp):
    query_blocks = queries.reshape(BLOCKS, BLK, D)
    passage_blocks = passages.reshape(BLOCKS, BLK, D)
    group_start = (jnp.arange(BLOCKS, dtype=jnp.int32) // GROUP) * GROUP
    global_ids = (block_lists + group_start[:, None]).astype(jnp.int32)
    listed = block_lists.shape[1]
    target = jnp.zeros((listed, BLK, BLK), jnp.float32).at[0].set(jnp.eye(BLK, dtype=jnp.float32))

    def one_block(accum, scanned):
        query_rows, block_ids = scanned
        key_rows = passage_blocks[block_ids]
        logits = inv_temp * jnp.einsum("qd,mkd->mqk", query_rows.astype(jnp.float32), key_rows.astype(jnp.float32), precision=lax.Precision.HIGHEST)
        row_peak = jnp.max(logits, axis=(0, 2))
        exp_terms = jnp.exp(logits - row_peak[None, :, None])
        exp_total = jnp.sum(exp_terms, axis=(0, 2))
        row_loss = row_peak + jnp.log(exp_total) - jnp.diagonal(logits[0])
        residual = exp_terms / exp_total[None, :, None] - target
        weights = residual.astype(jnp.bfloat16)
        query_grad = (inv_temp * jnp.einsum("mqk,mkd->qd", weights.astype(jnp.float32), key_rows.astype(jnp.float32), precision=lax.Precision.HIGHEST)).astype(jnp.bfloat16)
        block_grad = (inv_temp * jnp.einsum("mqk,qd->mkd", weights.astype(jnp.float32), query_rows.astype(jnp.float32), precision=lax.Precision.HIGHEST)).astype(jnp.bfloat16)
        accum = accum.at[block_ids].add(block_grad.astype(jnp.float32))
        temp_term = jnp.sum(residual * logits) / inv_temp
        return accum, (query_grad, jnp.sum(row_loss), temp_term)

    start_accum = jnp.zeros((BLOCKS, BLK, D), jnp.float32)
    accum, (query_grads, loss_sums, temp_terms) = lax.scan(one_block, start_accum, (query_blocks, global_ids))
    query_grad = query_grads.reshape(TOKENS, D)
    passage_grad = accum.astype(jnp.bfloat16).reshape(TOKENS, D)
    return (query_grad, passage_grad, jnp.sum(loss_sums) / TOKENS, jnp.sum(temp_terms) / TOKENS)
```

```python
import functools

import jax
import jax.numpy as jnp
from jax import lax
from jax.experimental import pallas as pl
from jax.experimental.pallas import tpu as pltpu
from jax.sharding import PartitionSpec as P

MESH = pl.DeviceIdType.MESH
LOW = -1e30
NT = (((1,), (1,)), ((), ()))
TN = (((0,), (0,)), ((), ()))
NN = (((1,), (0,)), ((), ()))


def dot(a, b, dims):
    return lax.dot_general(a, b, dims, preferred_element_type=jnp.float32)


def kernel(line, groups, q_in, p_in, lists, temp, qg_out, pg_out, tot_out,
           pcol, qcat, ebuf, wbuf, mrec, stat, stat_in, chip_in, own, zin_r, zin_l,
           zsend, psend, qsend, qrecv, acc, acc_in,
           loc_sem, q_sems, p_recv, p_right, p_left, p_core, st_sems,
           c_send, c_recv, r_send, r_recv, l_send, l_recv, g_sems, a_send, a_recv):
    rows = q_in.shape[0]
    listed = lists.shape[1]
    dp = lax.axis_index("dp")
    me = lax.axis_index("shard")
    k = lax.rem(me, 2)
    x = lax.rem(me // 2, 2)
    z = me // 4

    def dev(zz, xx, kk):
        return (dp, (zz * 2 + xx) * 2 + kk)

    core = dev(z, x, 1 - k)
    mate = dev(z, 1 - x, k)
    right = dev(lax.rem(z + 1, line), x, k)
    left = dev(lax.rem(z + line - 1, line), x, k)
    has_r = z < line - 1
    has_l = z > 0
    pairs = [core, mate]
    bit = 1
    far = []
    while bit < line:
        other = z + bit - 2 * bit * lax.rem(z // bit, 2)
        pairs.append(dev(other, x, k))
        if bit > 1:
            far.append(dev(other, x, k))
        bit *= 2
    bit = 1
    while bit < groups:
        other = dp + bit - 2 * bit * lax.rem(dp // bit, 2)
        pairs.append((other, me))
        far.append((other, me))
        bit *= 2

    mine = z * 2 + k
    own_p = pltpu.make_async_copy(p_in, pcol.at[mine], loc_sem.at[0])
    own_q = pltpu.make_async_copy(q_in, qcat.at[pl.ds(x * rows, rows)], loc_sem.at[1])
    own_p.start()
    own_q.start()

    barrier = pltpu.get_barrier_semaphore()
    for d in [core, mate] + far:
        pl.semaphore_signal(barrier, inc=1, device_id=d, device_id_type=MESH)

    @pl.when(has_r)
    def _():
        pl.semaphore_signal(barrier, inc=1, device_id=right, device_id_type=MESH)

    @pl.when(has_l)
    def _():
        pl.semaphore_signal(barrier, inc=1, device_id=left, device_id_type=MESH)

    ends = jnp.where(has_r, 1, 0) + jnp.where(has_l, 1, 0)
    pl.semaphore_wait(barrier, 2 + len(far) + ends)

    def remote(src, dst, send, recv, d):
        return pltpu.make_async_remote_copy(
            src_ref=src, dst_ref=dst, send_sem=send, recv_sem=recv,
            device_id=d, device_id_type=MESH)

    def p_copy(zz, sems, d):
        slot = zz * 2 + k
        return remote(pcol.at[slot], pcol.at[slot], sems.at[zz], p_recv.at[slot], d)

    def p_wait(slot):
        remote(pcol.at[slot], pcol.at[slot], p_core.at[0], p_recv.at[slot], core).wait_recv()

    my_rows = pl.ds(x * rows, rows)
    q_copy = remote(qcat.at[my_rows], qcat.at[my_rows], q_sems.at[0], q_sems.at[1], mate)
    mate_rows = pl.ds((1 - x) * rows, rows)
    q_wait = remote(qcat.at[mate_rows], qcat.at[mate_rows], q_sems.at[0], q_sems.at[1], mate)

    own_p.wait()

    @pl.when(has_r)
    def _():
        p_copy(z, p_right, right).start()

    @pl.when(has_l)
    def _():
        p_copy(z, p_left, left).start()

    own_q.wait()
    q_copy.start()
    p_copy(z, p_core, core).start()

    lane = lax.broadcasted_iota(jnp.int32, (1, 2 * rows), 1)
    jj = lax.broadcasted_iota(jnp.int32, (rows, 2 * rows), 0)
    ii = lax.broadcasted_iota(jnp.int32, (rows, 2 * rows), 1)
    eye = jj == jnp.where(ii < rows, ii, ii - rows)
    inv_temp = temp[0]
    row_a = z * 4 + k
    row_b = z * 4 + 2 + k

    def per_lane(block_id, first, last):
        a = jnp.int32(0)
        b = jnp.int32(0)
        for m in range(first, last):
            a = a + jnp.where(lists[row_a, m] == block_id, 1, 0)
            b = b + jnp.where(lists[row_b, m] == block_id, 1, 0)
        return jnp.where(lane < rows, a, b)

    def block_of(slot):
        return (slot // 2) * 4 + x * 2 + lax.rem(slot, 2)

    stat[0:1, :] = jnp.full((1, 2 * rows), LOW, jnp.float32)
    stat[1:8, :] = jnp.zeros((7, 2 * rows), jnp.float32)

    def consume(slot):
        ident = block_of(slot)
        live = per_lane(ident, 0, listed) > 0
        pos = per_lane(ident, 0, 1) > 0
        s = dot(pcol[slot], qcat[...], NT) * inv_temp
        s = jnp.where(live, s, LOW)
        m_old = stat[0:1, :]
        m_new = jnp.maximum(m_old, jnp.max(s, axis=0, keepdims=True))
        e = jnp.exp(s - m_new)
        ebuf[slot] = e
        scale = jnp.exp(m_old - m_new)
        stat[0:1, :] = m_new
        stat[1:2, :] = stat[1:2, :] * scale + jnp.sum(e, axis=0, keepdims=True)
        stat[2:3, :] = stat[2:3, :] * scale + jnp.sum(e * s, axis=0, keepdims=True)
        diag = jnp.sum(jnp.where(eye, s, 0.0), axis=0, keepdims=True)
        stat[3:4, :] = stat[3:4, :] + jnp.where(pos, diag, 0.0)
        mrec[slot] = jnp.broadcast_to(m_new, (8, 2 * rows))

    q_wait.wait_recv()

    @pl.loop(0, line - 1)
    def _(s):
        from_l = z - 1 - s
        from_r = z + 1 + s

        @pl.when(from_l >= 0)
        def _():
            p_wait(from_l * 2 + k)

            @pl.when(has_r)
            def _():
                p_copy(from_l, p_right, right).start()

            p_copy(from_l, p_core, core).start()

        @pl.when(from_r < line)
        def _():
            p_wait(from_r * 2 + k)

            @pl.when(has_l)
            def _():
                p_copy(from_r, p_left, left).start()

            p_copy(from_r, p_core, core).start()

        @pl.when(s == 0)
        def _():
            consume(mine)
            p_wait(z * 2 + 1 - k)
            consume(z * 2 + 1 - k)

        @pl.when(from_l >= 0)
        def _():
            consume(from_l * 2 + k)
            p_wait(from_l * 2 + 1 - k)
            consume(from_l * 2 + 1 - k)

        @pl.when(from_r < line)
        def _():
            consume(from_r * 2 + k)
            p_wait(from_r * 2 + 1 - k)
            consume(from_r * 2 + 1 - k)

    st_copy = remote(stat, stat_in, st_sems.at[0], st_sems.at[1], mate)
    st_copy.start()
    st_copy.wait_recv()
    m_loc = stat[0:1, :]
    m_in = stat_in[0:1, :]
    peak = jnp.maximum(m_loc, m_in)
    total = stat[1:2, :] * jnp.exp(m_loc - peak) + stat_in[1:2, :] * jnp.exp(m_in - peak)
    inv_total = 1.0 / total

    def make_w(slot):
        pos = per_lane(block_of(slot), 0, 1) > 0
        scale = jnp.exp(mrec[slot][0:1, :] - peak) * inv_total
        target = jnp.where(jnp.logical_and(eye, pos), 1.0, 0.0)
        w = (ebuf[slot] * scale - target).astype(jnp.bfloat16)
        wbuf[slot] = w
        return w

    def p_grad(slot):
        return dot(make_w(slot), qcat[...], NN) * inv_temp

    def c_copy(d):
        return remote(psend.at[d], chip_in.at[d], c_send.at[d], c_recv.at[d], core)

    def r_copy(d):
        return remote(zsend.at[d], zin_r.at[d], r_send.at[d], r_recv.at[d], right)

    def l_copy(d):
        return remote(zsend.at[d], zin_l.at[d], l_send.at[d], l_recv.at[d], left)

    def give(d):
        psend[d] = p_grad(d * 2 + 1 - k).astype(jnp.bfloat16)
        c_copy(d).start()

    def take(d):
        own[d] = p_grad(d * 2 + k)
        c_copy(d).wait_recv()
        own[d] = own[d] + chip_in[d].astype(jnp.float32)

    @pl.loop(0, line - 1)
    def _(s):
        dr = line - 1 - s
        dl = s

        @pl.when(dr > z)
        def _():
            give(dr)

        @pl.when(dl < z)
        def _():
            give(dl)

        @pl.when(dr > z)
        def _():
            take(dr)

            @pl.when(z == 0)
            def _():
                zsend[dr] = own[dr].astype(jnp.bfloat16)
                r_copy(dr).start()

        @pl.when(dl < z)
        def _():
            take(dl)

            @pl.when(z == line - 1)
            def _():
                zsend[dl] = own[dl].astype(jnp.bfloat16)
                l_copy(dl).start()

    give(z)
    take(z)

    def q_part(start):
        part = jnp.zeros((rows, q_in.shape[1]), jnp.float32)
        for c in range(2 * line):
            part = part + dot(wbuf[c, :, pl.ds(start, rows)], pcol[c], TN)
        return part * inv_temp

    @pl.when(x == 0)
    def _():
        qsend[...] = q_part(rows).astype(jnp.bfloat16)

    @pl.when(x == 1)
    def _():
        qsend[...] = q_part(0).astype(jnp.bfloat16)

    g_copy = remote(qsend, qrecv, g_sems.at[0], g_sems.at[1], mate)
    g_copy.start()

    owner = (lane >= x * rows) & (lane < x * rows + rows)
    diag = stat[3:4, :]
    loss = jnp.where(owner, peak + jnp.log(total), 0.0) - diag
    grad = stat[2:3, :] * (jnp.exp(m_loc - peak) * inv_total) - diag
    loss = jnp.sum(loss, axis=1, keepdims=True)
    grad = jnp.sum(grad, axis=1, keepdims=True) / inv_temp
    tile_row = lax.broadcasted_iota(jnp.int32, (8, 128), 0)
    acc[0] = jnp.where(tile_row == 0, loss, grad)
    a_copies = []
    for i, d in enumerate(pairs):
        copy = remote(acc.at[i], acc_in.at[i], a_send.at[i], a_recv.at[i], d)
        copy.start()
        copy.wait_recv()
        acc[i + 1] = acc[i] + acc_in[i]
        a_copies.append(copy)
    tot_out[...] = acc[len(pairs)]

    @pl.when(x == 0)
    def _():
        qg_out[...] = q_part(0).astype(jnp.bfloat16)

    @pl.when(x == 1)
    def _():
        qg_out[...] = q_part(rows).astype(jnp.bfloat16)

    @pl.loop(0, line - 1)
    def _(s):
        dr = line - 1 - s
        dl = s

        @pl.when((dr > z) & has_l)
        def _():
            r_copy(dr).wait_recv()
            zsend[dr] = (own[dr] + zin_r[dr].astype(jnp.float32)).astype(jnp.bfloat16)
            r_copy(dr).start()

        @pl.when((dl < z) & has_r)
        def _():
            l_copy(dl).wait_recv()
            zsend[dl] = (own[dl] + zin_l[dl].astype(jnp.float32)).astype(jnp.bfloat16)
            l_copy(dl).start()

    g_copy.wait_recv()
    qg_out[...] = (qg_out[...].astype(jnp.float32) + qrecv[...].astype(jnp.float32)).astype(jnp.bfloat16)

    @pl.when(has_l)
    def _():
        r_copy(z).wait_recv()
        own[z] = own[z] + zin_r[z].astype(jnp.float32)

    @pl.when(has_r)
    def _():
        l_copy(z).wait_recv()
        own[z] = own[z] + zin_l[z].astype(jnp.float32)

    pg_out[...] = own[z].astype(jnp.bfloat16)

    q_copy.wait_send()
    st_copy.wait_send()
    g_copy.wait_send()
    for copy in a_copies:
        copy.wait_send()

    @pl.loop(0, line)
    def _(d):
        p_copy(d, p_core, core).wait_send()
        c_copy(d).wait_send()

        @pl.when((d <= z) & has_r)
        def _():
            p_copy(d, p_right, right).wait_send()

        @pl.when((d >= z) & has_l)
        def _():
            p_copy(d, p_left, left).wait_send()

        @pl.when(d > z)
        def _():
            r_copy(d).wait_send()

        @pl.when(d < z)
        def _():
            l_copy(d).wait_send()


def fused(line, groups, queries, passages, block_lists, inv_temp):
    rows, width = passages.shape
    stages = 2 + (line.bit_length() - 1) + (groups.bit_length() - 1)
    bf, f32 = jnp.bfloat16, jnp.float32
    block = (rows, width)
    vm, dma = pltpu.VMEM, pltpu.SemaphoreType.DMA
    scratch = [
        vm((2 * line,) + block, bf),
        vm((2 * rows, width), bf),
        vm((2 * line, rows, 2 * rows), f32),
        vm((2 * line, rows, 2 * rows), bf),
        vm((2 * line, 8, 2 * rows), f32),
        vm((8, 2 * rows), f32),
        vm((8, 2 * rows), f32),
        vm((line,) + block, bf),
        vm((line,) + block, f32),
        vm((line,) + block, bf),
        vm((line,) + block, bf),
        vm((line,) + block, bf),
        vm((line,) + block, bf),
        vm(block, bf),
        vm(block, bf),
        vm((stages + 1, 8, 128), f32),
        vm((stages, 8, 128), f32),
        dma((2,)), dma((2,)), dma((2 * line,)), dma((line,)), dma((line,)), dma((line,)), dma((2,)),
        dma((line,)), dma((line,)), dma((line,)), dma((line,)), dma((line,)), dma((line,)),
        dma((2,)), dma((stages,)), dma((stages,)),
    ]
    query_grad, passage_grad, totals = pl.pallas_call(
        functools.partial(kernel, line, groups),
        out_shape=(
            jax.ShapeDtypeStruct(block, bf),
            jax.ShapeDtypeStruct(block, bf),
            jax.ShapeDtypeStruct((8, 128), f32),
        ),
        in_specs=[
            pl.BlockSpec(memory_space=pl.ANY),
            pl.BlockSpec(memory_space=pl.ANY),
            pl.BlockSpec(memory_space=pltpu.SMEM),
            pl.BlockSpec(memory_space=pltpu.SMEM),
        ],
        out_specs=(pl.BlockSpec(memory_space=pltpu.VMEM),) * 3,
        scratch_shapes=scratch,
        compiler_params=pltpu.CompilerParams(
            collective_id=0, has_side_effects=True, vmem_limit_bytes=56 * 1024 * 1024
        ),
    )(queries, passages, block_lists, inv_temp.reshape(1))
    pair_count = rows * groups * line * 4
    return query_grad, passage_grad, totals[0, 0] / pair_count, totals[1, 0] / pair_count


def plain(queries, passages, block_lists, inv_temp):
    shard_count = lax.axis_size("shard")
    row_count, feat_width = passages.shape
    listed = block_lists.shape[1]
    col_piece = feat_width // shard_count
    outgoing = passages.reshape(row_count, shard_count, col_piece).transpose(1, 0, 2)
    stripes = lax.all_to_all(outgoing, "shard", split_axis=0, concat_axis=0, tiled=True)
    requests = stripes[block_lists]
    fetched = lax.all_to_all(requests, "shard", split_axis=0, concat_axis=3, tiled=True)
    key_rows = fetched[0]
    logits = inv_temp * jnp.einsum(
        "qd,mkd->mqk", queries, key_rows, preferred_element_type=jnp.float32
    )
    row_peak = jnp.max(logits, axis=(0, 2))
    exp_terms = jnp.exp(logits - row_peak[None, :, None])
    exp_total = jnp.sum(exp_terms, axis=(0, 2))
    row_loss = row_peak + jnp.log(exp_total) - jnp.diagonal(logits[0])
    first_block = (jnp.arange(listed, dtype=jnp.int32) == 0).astype(jnp.float32)
    target = first_block[:, None, None] * jnp.eye(row_count, dtype=jnp.float32)[None]
    residual = exp_terms / exp_total[None, :, None] - target
    weights = residual.astype(jnp.bfloat16)
    temp_part = jnp.sum(residual * logits) / inv_temp
    block_grad = (
        inv_temp * jnp.einsum("mqk,qd->mkd", weights, queries, preferred_element_type=jnp.float32)
    ).astype(jnp.bfloat16)[None]
    query_grad = (
        inv_temp * jnp.einsum("mqk,mkd->qd", weights, key_rows, preferred_element_type=jnp.float32)
    ).astype(jnp.bfloat16)
    block_index = jnp.arange(shard_count, dtype=jnp.int32)
    onehot = (block_lists.reshape(-1)[None, :] == block_index[:, None]).astype(jnp.bfloat16)
    returned = lax.all_to_all(block_grad, "shard", split_axis=3, concat_axis=0, tiled=True)
    summed = jnp.dot(
        onehot,
        returned.reshape(shard_count * listed, row_count * col_piece),
        preferred_element_type=jnp.float32,
    )
    settled = summed.astype(jnp.bfloat16).reshape(shard_count, row_count, col_piece)
    arrived = lax.all_to_all(settled, "shard", split_axis=0, concat_axis=0, tiled=True)
    passage_grad = arrived.transpose(1, 0, 2).reshape(row_count, feat_width)
    totals = lax.psum((jnp.sum(row_loss), temp_part), ("dp", "shard"))
    pair_count = row_count * lax.axis_size("dp") * shard_count
    return query_grad, passage_grad, totals[0] / pair_count, totals[1] / pair_count


def solution(mesh):
    shard_count, groups = mesh.shape["shard"], mesh.shape["dp"]
    line = shard_count // 4
    short = shard_count % 4 == 0 and 2 <= line <= 4 and line & (line - 1) == 0
    body = functools.partial(fused, line, groups) if short and groups & (groups - 1) == 0 else plain
    placed = (P(("dp", "shard"), None), P(("dp", "shard"), None), P("dp", None), P())
    return jax.shard_map(
        body,
        mesh=mesh,
        in_specs=placed,
        out_specs=(P(("dp", "shard"), None), P(("dp", "shard"), None), P(), P()),
        check_vma=False,
    )
```

```python
import functools

import jax
import jax.numpy as jnp
from jax import lax
from jax.experimental import pallas as pl
from jax.experimental.pallas import tpu as pltpu
from jax.sharding import PartitionSpec as P

MESH = pl.DeviceIdType.MESH
LOW = -1e30
NT = (((1,), (1,)), ((), ()))
TN = (((0,), (0,)), ((), ()))
NN = (((1,), (0,)), ((), ()))


def dot(a, b, dims):
    return lax.dot_general(a, b, dims, preferred_element_type=jnp.float32)


def kernel(line, groups, q_in, p_in, lists, temp, qg_out, pg_out, tot_out,
           pcol, qcat, ebuf, wbuf, mrec, stat, stat_in, chip_in, own, zin_r, zin_l,
           zsend, psend, qsend, qrecv, acc, acc_in,
           loc_sem, q_sems, p_recv, p_right, p_left, p_core, st_sems,
           c_send, c_recv, r_send, r_recv, l_send, l_recv, g_sems, a_send, a_recv):
    rows = q_in.shape[0]
    listed = lists.shape[1]
    dp = lax.axis_index("dp")
    me = lax.axis_index("shard")
    k = lax.rem(me, 2)
    x = lax.rem(me // 2, 2)
    z = me // 4

    def dev(zz, xx, kk):
        return (dp, (zz * 2 + xx) * 2 + kk)

    core = dev(z, x, 1 - k)
    mate = dev(z, 1 - x, k)
    right = dev(lax.rem(z + 1, line), x, k)
    left = dev(lax.rem(z + line - 1, line), x, k)
    has_r = z < line - 1
    has_l = z > 0
    pairs = [core, mate]
    bit = 1
    far = []
    while bit < line:
        other = z + bit - 2 * bit * lax.rem(z // bit, 2)
        pairs.append(dev(other, x, k))
        if bit > 1:
            far.append(dev(other, x, k))
        bit *= 2
    bit = 1
    while bit < groups:
        other = dp + bit - 2 * bit * lax.rem(dp // bit, 2)
        pairs.append((other, me))
        far.append((other, me))
        bit *= 2

    mine = z * 2 + k
    own_p = pltpu.make_async_copy(p_in, pcol.at[pl.ds(mine * rows, rows)], loc_sem.at[0])
    own_q = pltpu.make_async_copy(q_in, qcat.at[pl.ds(x * rows, rows)], loc_sem.at[1])
    own_p.start()
    own_q.start()

    barrier = pltpu.get_barrier_semaphore()
    for d in [core, mate] + far:
        pl.semaphore_signal(barrier, inc=1, device_id=d, device_id_type=MESH)

    @pl.when(has_r)
    def _():
        pl.semaphore_signal(barrier, inc=1, device_id=right, device_id_type=MESH)

    @pl.when(has_l)
    def _():
        pl.semaphore_signal(barrier, inc=1, device_id=left, device_id_type=MESH)

    ends = jnp.where(has_r, 1, 0) + jnp.where(has_l, 1, 0)
    pl.semaphore_wait(barrier, 2 + len(far) + ends)

    def remote(src, dst, send, recv, d):
        return pltpu.make_async_remote_copy(
            src_ref=src, dst_ref=dst, send_sem=send, recv_sem=recv,
            device_id=d, device_id_type=MESH)

    def p_copy(zz, sems, d):
        slot = zz * 2 + k
        span = pcol.at[pl.ds(slot * rows, rows)]
        return remote(span, span, sems.at[zz], p_recv.at[slot], d)

    def p_wait(slot):
        span = pcol.at[pl.ds(slot * rows, rows)]
        remote(span, span, p_core.at[0], p_recv.at[slot], core).wait_recv()

    my_rows = pl.ds(x * rows, rows)
    q_copy = remote(qcat.at[my_rows], qcat.at[my_rows], q_sems.at[0], q_sems.at[1], mate)
    mate_rows = pl.ds((1 - x) * rows, rows)
    q_wait = remote(qcat.at[mate_rows], qcat.at[mate_rows], q_sems.at[0], q_sems.at[1], mate)

    own_p.wait()

    @pl.when(has_r)
    def _():
        p_copy(z, p_right, right).start()

    @pl.when(has_l)
    def _():
        p_copy(z, p_left, left).start()

    own_q.wait()
    q_copy.start()
    p_copy(z, p_core, core).start()

    lane = lax.broadcasted_iota(jnp.int32, (1, 2 * rows), 1)
    jj = lax.broadcasted_iota(jnp.int32, (rows, 2 * rows), 0)
    ii = lax.broadcasted_iota(jnp.int32, (rows, 2 * rows), 1)
    eye = jj == jnp.where(ii < rows, ii, ii - rows)
    inv_temp = temp[0]
    row_a = z * 4 + k
    row_b = z * 4 + 2 + k

    def per_lane(block_id, first, last):
        a = jnp.int32(0)
        b = jnp.int32(0)
        for m in range(first, last):
            a = a + jnp.where(lists[row_a, m] == block_id, 1, 0)
            b = b + jnp.where(lists[row_b, m] == block_id, 1, 0)
        return jnp.where(lane < rows, a, b)

    def block_of(slot):
        return (slot // 2) * 4 + x * 2 + lax.rem(slot, 2)

    stat[0:1, :] = jnp.full((1, 2 * rows), LOW, jnp.float32)
    stat[1:8, :] = jnp.zeros((7, 2 * rows), jnp.float32)

    def consume(slot):
        ident = block_of(slot)
        live = per_lane(ident, 0, listed) > 0
        pos = per_lane(ident, 0, 1) > 0
        s = dot(pcol[pl.ds(slot * rows, rows)], qcat[...], NT) * inv_temp
        s = jnp.where(live, s, LOW)
        m_old = stat[0:1, :]
        m_new = jnp.maximum(m_old, jnp.max(s, axis=0, keepdims=True))
        e = jnp.exp(s - m_new)
        ebuf[slot] = e
        scale = jnp.exp(m_old - m_new)
        stat[0:1, :] = m_new
        stat[1:2, :] = stat[1:2, :] * scale + jnp.sum(e, axis=0, keepdims=True)
        stat[2:3, :] = stat[2:3, :] * scale + jnp.sum(e * s, axis=0, keepdims=True)
        diag = jnp.sum(jnp.where(eye, s, 0.0), axis=0, keepdims=True)
        stat[3:4, :] = stat[3:4, :] + jnp.where(pos, diag, 0.0)
        mrec[slot] = jnp.broadcast_to(m_new, (8, 2 * rows))

    def take_pair(zz):
        consume(zz * 2 + k)
        p_wait(zz * 2 + 1 - k)
        consume(zz * 2 + 1 - k)

    q_wait.wait_recv()

    @pl.loop(0, line - 1)
    def _(s):
        from_l = z - 1 - s
        from_r = z + 1 + s

        @pl.when(from_l >= 0)
        def _():
            p_wait(from_l * 2 + k)

            @pl.when(has_r)
            def _():
                p_copy(from_l, p_right, right).start()

            p_copy(from_l, p_core, core).start()

        @pl.when(from_r < line)
        def _():
            p_wait(from_r * 2 + k)

            @pl.when(has_l)
            def _():
                p_copy(from_r, p_left, left).start()

            p_copy(from_r, p_core, core).start()

        @pl.when(s == 0)
        def _():
            consume(mine)
            p_wait(z * 2 + 1 - k)
            consume(z * 2 + 1 - k)

        @pl.when((s > 0) & (from_l + 1 >= 0) & (from_r - 1 < line))
        def _():
            take_pair(from_r - 1)

        @pl.when(from_l >= 0)
        def _():
            take_pair(from_l)

        @pl.when((from_r < line) & (from_l < 0))
        def _():
            take_pair(from_r)

    st_copy = remote(stat, stat_in, st_sems.at[0], st_sems.at[1], mate)
    st_copy.start()
    st_copy.wait_recv()
    m_loc = stat[0:1, :]
    m_in = stat_in[0:1, :]
    peak = jnp.maximum(m_loc, m_in)
    total = stat[1:2, :] * jnp.exp(m_loc - peak) + stat_in[1:2, :] * jnp.exp(m_in - peak)
    inv_total = 1.0 / total

    def make_w(slot):
        pos = per_lane(block_of(slot), 0, 1) > 0
        scale = jnp.exp(mrec[slot][0:1, :] - peak) * inv_total
        target = jnp.where(jnp.logical_and(eye, pos), 1.0, 0.0)
        w = (ebuf[slot] * scale - target).astype(jnp.bfloat16)
        wbuf[pl.ds(slot * rows, rows)] = w
        return w

    def p_grad(slot):
        return dot(make_w(slot), qcat[...], NN) * inv_temp

    def c_copy(d):
        return remote(psend.at[d], chip_in.at[d], c_send.at[d], c_recv.at[d], core)

    def r_copy(d):
        return remote(zsend.at[d], zin_r.at[d], r_send.at[d], r_recv.at[d], right)

    def l_copy(d):
        return remote(zsend.at[d], zin_l.at[d], l_send.at[d], l_recv.at[d], left)

    def give(d):
        psend[d] = p_grad(d * 2 + 1 - k).astype(jnp.bfloat16)
        c_copy(d).start()

    def take(d):
        own[d] = p_grad(d * 2 + k)
        c_copy(d).wait_recv()
        own[d] = own[d] + chip_in[d].astype(jnp.float32)

    @pl.loop(0, line - 1)
    def _(s):
        dr = line - 1 - s
        dl = s

        @pl.when(dr > z)
        def _():
            give(dr)

        @pl.when(dl < z)
        def _():
            give(dl)

        @pl.when(dr > z)
        def _():
            take(dr)

            @pl.when(z == 0)
            def _():
                zsend[dr] = own[dr].astype(jnp.bfloat16)
                r_copy(dr).start()

        @pl.when(dl < z)
        def _():
            take(dl)

            @pl.when(z == line - 1)
            def _():
                zsend[dl] = own[dl].astype(jnp.bfloat16)
                l_copy(dl).start()

    give(z)
    take(z)

    def q_part(start):
        return dot(wbuf[:, pl.ds(start, rows)], pcol[...], TN) * inv_temp

    def pass_on(t):
        dr = line - 1 + z - t
        dl = t - (line - 1 - z)

        @pl.when((dr > z) & (dr < line) & has_l)
        def _():
            r_copy(dr).wait_recv()
            zsend[dr] = (own[dr] + zin_r[dr].astype(jnp.float32)).astype(jnp.bfloat16)
            r_copy(dr).start()

        @pl.when((dl < z) & (dl >= 0) & has_r)
        def _():
            l_copy(dl).wait_recv()
            zsend[dl] = (own[dl] + zin_l[dl].astype(jnp.float32)).astype(jnp.bfloat16)
            l_copy(dl).start()

    if line > 2:
        pass_on(1)

    @pl.when(x == 0)
    def _():
        qsend[...] = q_part(rows).astype(jnp.bfloat16)

    @pl.when(x == 1)
    def _():
        qsend[...] = q_part(0).astype(jnp.bfloat16)

    g_copy = remote(qsend, qrecv, g_sems.at[0], g_sems.at[1], mate)
    g_copy.start()

    @pl.loop(2, line - 1)
    def _(t):
        pass_on(t)

    @pl.when(x == 0)
    def _():
        qg_out[...] = q_part(0).astype(jnp.bfloat16)

    @pl.when(x == 1)
    def _():
        qg_out[...] = q_part(rows).astype(jnp.bfloat16)

    own_lane = (lane >= x * rows) & (lane < x * rows + rows)
    diag = stat[3:4, :]
    loss = jnp.where(own_lane, peak + jnp.log(total), 0.0) - diag
    grad = stat[2:3, :] * (jnp.exp(m_loc - peak) * inv_total) - diag
    loss = jnp.sum(loss, axis=1, keepdims=True)
    grad = jnp.sum(grad, axis=1, keepdims=True) / inv_temp
    tile_row = lax.broadcasted_iota(jnp.int32, (8, 128), 0)
    acc[0] = jnp.where(tile_row == 0, loss, grad)
    a_copies = []
    for i, d in enumerate(pairs):
        copy = remote(acc.at[i], acc_in.at[i], a_send.at[i], a_recv.at[i], d)
        copy.start()
        copy.wait_recv()
        acc[i + 1] = acc[i] + acc_in[i]
        a_copies.append(copy)
    tot_out[...] = acc[len(pairs)]

    g_copy.wait_recv()
    qg_out[...] = (qg_out[...].astype(jnp.float32) + qrecv[...].astype(jnp.float32)).astype(jnp.bfloat16)

    @pl.when(has_l)
    def _():
        r_copy(z).wait_recv()
        own[z] = own[z] + zin_r[z].astype(jnp.float32)

    @pl.when(has_r)
    def _():
        l_copy(z).wait_recv()
        own[z] = own[z] + zin_l[z].astype(jnp.float32)

    pg_out[...] = own[z].astype(jnp.bfloat16)

    q_copy.wait_send()
    st_copy.wait_send()
    g_copy.wait_send()
    for copy in a_copies:
        copy.wait_send()

    @pl.loop(0, line)
    def _(d):
        p_copy(d, p_core, core).wait_send()
        c_copy(d).wait_send()

        @pl.when((d <= z) & has_r)
        def _():
            p_copy(d, p_right, right).wait_send()

        @pl.when((d >= z) & has_l)
        def _():
            p_copy(d, p_left, left).wait_send()

        @pl.when(d > z)
        def _():
            r_copy(d).wait_send()

        @pl.when(d < z)
        def _():
            l_copy(d).wait_send()


def fused(line, groups, queries, passages, block_lists, inv_temp):
    rows, width = passages.shape
    stages = 2 + (line.bit_length() - 1) + (groups.bit_length() - 1)
    bf, f32 = jnp.bfloat16, jnp.float32
    block = (rows, width)
    vm, dma = pltpu.VMEM, pltpu.SemaphoreType.DMA
    scratch = [
        vm((2 * line * rows, width), bf),
        vm((2 * rows, width), bf),
        vm((2 * line, rows, 2 * rows), f32),
        vm((2 * line * rows, 2 * rows), bf),
        vm((2 * line, 8, 2 * rows), f32),
        vm((8, 2 * rows), f32),
        vm((8, 2 * rows), f32),
        vm((line,) + block, bf),
        vm((line,) + block, f32),
        vm((line,) + block, bf),
        vm((line,) + block, bf),
        vm((line,) + block, bf),
        vm((line,) + block, bf),
        vm(block, bf),
        vm(block, bf),
        vm((stages + 1, 8, 128), f32),
        vm((stages, 8, 128), f32),
        dma((2,)), dma((2,)), dma((2 * line,)), dma((line,)), dma((line,)), dma((line,)), dma((2,)),
        dma((line,)), dma((line,)), dma((line,)), dma((line,)), dma((line,)), dma((line,)),
        dma((2,)), dma((stages,)), dma((stages,)),
    ]
    query_grad, passage_grad, totals = pl.pallas_call(
        functools.partial(kernel, line, groups),
        out_shape=(
            jax.ShapeDtypeStruct(block, bf),
            jax.ShapeDtypeStruct(block, bf),
            jax.ShapeDtypeStruct((8, 128), f32),
        ),
        in_specs=[
            pl.BlockSpec(memory_space=pl.ANY),
            pl.BlockSpec(memory_space=pl.ANY),
            pl.BlockSpec(memory_space=pltpu.SMEM),
            pl.BlockSpec(memory_space=pltpu.SMEM),
        ],
        out_specs=(pl.BlockSpec(memory_space=pltpu.VMEM),) * 3,
        scratch_shapes=scratch,
        compiler_params=pltpu.CompilerParams(
            collective_id=0, has_side_effects=True, vmem_limit_bytes=56 * 1024 * 1024
        ),
    )(queries, passages, block_lists, inv_temp.reshape(1))
    pair_count = rows * groups * line * 4
    return query_grad, passage_grad, totals[0, 0] / pair_count, totals[1, 0] / pair_count


def plain(queries, passages, block_lists, inv_temp):
    shard_count = lax.axis_size("shard")
    row_count, feat_width = passages.shape
    listed = block_lists.shape[1]
    col_piece = feat_width // shard_count
    outgoing = passages.reshape(row_count, shard_count, col_piece).transpose(1, 0, 2)
    stripes = lax.all_to_all(outgoing, "shard", split_axis=0, concat_axis=0, tiled=True)
    requests = stripes[block_lists]
    fetched = lax.all_to_all(requests, "shard", split_axis=0, concat_axis=3, tiled=True)
    key_rows = fetched[0]
    logits = inv_temp * jnp.einsum(
        "qd,mkd->mqk", queries, key_rows, preferred_element_type=jnp.float32
    )
    row_peak = jnp.max(logits, axis=(0, 2))
    exp_terms = jnp.exp(logits - row_peak[None, :, None])
    exp_total = jnp.sum(exp_terms, axis=(0, 2))
    row_loss = row_peak + jnp.log(exp_total) - jnp.diagonal(logits[0])
    first_block = (jnp.arange(listed, dtype=jnp.int32) == 0).astype(jnp.float32)
    target = first_block[:, None, None] * jnp.eye(row_count, dtype=jnp.float32)[None]
    residual = exp_terms / exp_total[None, :, None] - target
    weights = residual.astype(jnp.bfloat16)
    temp_part = jnp.sum(residual * logits) / inv_temp
    block_grad = (
        inv_temp * jnp.einsum("mqk,qd->mkd", weights, queries, preferred_element_type=jnp.float32)
    ).astype(jnp.bfloat16)[None]
    query_grad = (
        inv_temp * jnp.einsum("mqk,mkd->qd", weights, key_rows, preferred_element_type=jnp.float32)
    ).astype(jnp.bfloat16)
    block_index = jnp.arange(shard_count, dtype=jnp.int32)
    onehot = (block_lists.reshape(-1)[None, :] == block_index[:, None]).astype(jnp.bfloat16)
    returned = lax.all_to_all(block_grad, "shard", split_axis=3, concat_axis=0, tiled=True)
    summed = jnp.dot(
        onehot,
        returned.reshape(shard_count * listed, row_count * col_piece),
        preferred_element_type=jnp.float32,
    )
    settled = summed.astype(jnp.bfloat16).reshape(shard_count, row_count, col_piece)
    arrived = lax.all_to_all(settled, "shard", split_axis=0, concat_axis=0, tiled=True)
    passage_grad = arrived.transpose(1, 0, 2).reshape(row_count, feat_width)
    totals = lax.psum((jnp.sum(row_loss), temp_part), ("dp", "shard"))
    pair_count = row_count * lax.axis_size("dp") * shard_count
    return query_grad, passage_grad, totals[0] / pair_count, totals[1] / pair_count


def solution(mesh):
    shard_count, groups = mesh.shape["shard"], mesh.shape["dp"]
    line = shard_count // 4
    short = shard_count % 4 == 0 and 2 <= line <= 4 and line & (line - 1) == 0
    body = functools.partial(fused, line, groups) if short and groups & (groups - 1) == 0 else plain
    placed = (P(("dp", "shard"), None), P(("dp", "shard"), None), P("dp", None), P())
    return jax.shard_map(
        body,
        mesh=mesh,
        in_specs=placed,
        out_specs=(P(("dp", "shard"), None), P(("dp", "shard"), None), P(), P()),
        check_vma=False,
    )
```

```python
import functools

import jax
import jax.numpy as jnp
from jax import lax
from jax.experimental import pallas as pl
from jax.experimental.pallas import tpu as pltpu
from jax.sharding import PartitionSpec as P

MESH = pl.DeviceIdType.MESH
LOW = -1e30
NT = (((1,), (1,)), ((), ()))
TN = (((0,), (0,)), ((), ()))
NN = (((1,), (0,)), ((), ()))
CUT = 2


def dot(a, b, dims):
    return lax.dot_general(a, b, dims, preferred_element_type=jnp.float32)


def kernel(line, groups, q_in, p_in, lists, temp, qg_out, pg_out, tot_out,
           pcol, qcat, ebuf, wbuf, mrec, stat, stat_in, chip_in, own, zin_r, zin_l,
           zsend, psend, qsend, qrecv, acc, acc_in,
           loc_sem, q_sems, p_recv, p_right, p_left, p_core, st_sems,
           c_send, c_recv, r_send, r_recv, l_send, l_recv, g_sems, a_send, a_recv):
    rows = q_in.shape[0]
    listed = lists.shape[1]
    half = rows // CUT
    dp = lax.axis_index("dp")
    me = lax.axis_index("shard")
    k = lax.rem(me, 2)
    x = lax.rem(me // 2, 2)
    z = me // 4

    def dev(zz, xx, kk):
        return (dp, (zz * 2 + xx) * 2 + kk)

    core = dev(z, x, 1 - k)
    mate = dev(z, 1 - x, k)
    right = dev(lax.rem(z + 1, line), x, k)
    left = dev(lax.rem(z + line - 1, line), x, k)
    has_r = z < line - 1
    has_l = z > 0
    pairs = [core, mate]
    bit = 1
    far = []
    while bit < line:
        other = z + bit - 2 * bit * lax.rem(z // bit, 2)
        pairs.append(dev(other, x, k))
        if bit > 1:
            far.append(dev(other, x, k))
        bit *= 2
    bit = 1
    while bit < groups:
        other = dp + bit - 2 * bit * lax.rem(dp // bit, 2)
        pairs.append((other, me))
        far.append((other, me))
        bit *= 2

    mine = z * 2 + k
    own_p = pltpu.make_async_copy(p_in, pcol.at[pl.ds(mine * rows, rows)], loc_sem.at[0])
    own_q = pltpu.make_async_copy(q_in, qcat.at[pl.ds(x * rows, rows)], loc_sem.at[1])
    own_p.start()
    own_q.start()

    barrier = pltpu.get_barrier_semaphore()
    for d in [core, mate] + far:
        pl.semaphore_signal(barrier, inc=1, device_id=d, device_id_type=MESH)

    @pl.when(has_r)
    def _():
        pl.semaphore_signal(barrier, inc=1, device_id=right, device_id_type=MESH)

    @pl.when(has_l)
    def _():
        pl.semaphore_signal(barrier, inc=1, device_id=left, device_id_type=MESH)

    ends = jnp.where(has_r, 1, 0) + jnp.where(has_l, 1, 0)
    pl.semaphore_wait(barrier, 2 + len(far) + ends)

    def remote(src, dst, send, recv, d):
        return pltpu.make_async_remote_copy(
            src_ref=src, dst_ref=dst, send_sem=send, recv_sem=recv,
            device_id=d, device_id_type=MESH)

    def p_span(slot, c):
        return pcol.at[pl.ds(slot * rows + c * half, half)]

    def p_copy(zz, c, sems, d):
        slot = zz * 2 + k
        span = p_span(slot, c)
        return remote(span, span, sems.at[zz * CUT + c], p_recv.at[slot * CUT + c], d)

    def p_wait(slot, c):
        span = p_span(slot, c)
        remote(span, span, p_core.at[0], p_recv.at[slot * CUT + c], core).wait_recv()

    my_rows = pl.ds(x * rows, rows)
    q_copy = remote(qcat.at[my_rows], qcat.at[my_rows], q_sems.at[0], q_sems.at[1], mate)
    mate_rows = pl.ds((1 - x) * rows, rows)
    q_wait = remote(qcat.at[mate_rows], qcat.at[mate_rows], q_sems.at[0], q_sems.at[1], mate)

    own_p.wait()

    for c in range(CUT):
        @pl.when(has_r)
        def _(c=c):
            p_copy(z, c, p_right, right).start()

        @pl.when(has_l)
        def _(c=c):
            p_copy(z, c, p_left, left).start()

    own_q.wait()
    q_copy.start()
    for c in range(CUT):
        p_copy(z, c, p_core, core).start()

    lane = lax.broadcasted_iota(jnp.int32, (1, 2 * rows), 1)
    jj = lax.broadcasted_iota(jnp.int32, (half, 2 * rows), 0)
    ii = lax.broadcasted_iota(jnp.int32, (half, 2 * rows), 1)
    ahead = jnp.where(ii < rows, ii, ii - rows) - jj
    inv_temp = temp[0]
    row_a = z * 4 + k
    row_b = z * 4 + 2 + k

    def per_lane(block_id, first, last):
        a = jnp.int32(0)
        b = jnp.int32(0)
        for m in range(first, last):
            a = a + jnp.where(lists[row_a, m] == block_id, 1, 0)
            b = b + jnp.where(lists[row_b, m] == block_id, 1, 0)
        return jnp.where(lane < rows, a, b)

    def block_of(slot):
        return (slot // 2) * 4 + x * 2 + lax.rem(slot, 2)

    stat[0:1, :] = jnp.full((1, 2 * rows), LOW, jnp.float32)
    stat[1:8, :] = jnp.zeros((7, 2 * rows), jnp.float32)

    def consume(slot, c):
        part = slot * CUT + c
        ident = block_of(slot)
        live = per_lane(ident, 0, listed) > 0
        pos = per_lane(ident, 0, 1) > 0
        s = dot(pcol[pl.ds(slot * rows + c * half, half)], qcat[...], NT) * inv_temp
        s = jnp.where(live, s, LOW)
        m_old = stat[0:1, :]
        m_new = jnp.maximum(m_old, jnp.max(s, axis=0, keepdims=True))
        e = jnp.exp(s - m_new)
        ebuf[part] = e
        scale = jnp.exp(m_old - m_new)
        stat[0:1, :] = m_new
        stat[1:2, :] = stat[1:2, :] * scale + jnp.sum(e, axis=0, keepdims=True)
        stat[2:3, :] = stat[2:3, :] * scale + jnp.sum(e * s, axis=0, keepdims=True)
        diag = jnp.sum(jnp.where(ahead == c * half, s, 0.0), axis=0, keepdims=True)
        stat[3:4, :] = stat[3:4, :] + jnp.where(pos, diag, 0.0)
        mrec[part] = jnp.broadcast_to(m_new, (8, 2 * rows))

    def take_pair(zz, c):
        consume(zz * 2 + k, c)
        p_wait(zz * 2 + 1 - k, c)
        consume(zz * 2 + 1 - k, c)

    q_wait.wait_recv()

    @pl.loop(0, (line - 1) * CUT)
    def _(t):
        s = t // CUT
        c = lax.rem(t, CUT)
        from_l = z - 1 - s
        from_r = z + 1 + s

        @pl.when(from_l >= 0)
        def _():
            p_wait(from_l * 2 + k, c)

            @pl.when(has_r)
            def _():
                p_copy(from_l, c, p_right, right).start()

            p_copy(from_l, c, p_core, core).start()

        @pl.when(from_r < line)
        def _():
            p_wait(from_r * 2 + k, c)

            @pl.when(has_l)
            def _():
                p_copy(from_r, c, p_left, left).start()

            p_copy(from_r, c, p_core, core).start()

        @pl.when(s == 0)
        def _():
            take_pair(z, c)

        @pl.when((s > 0) & (from_l + 1 >= 0) & (from_r - 1 < line))
        def _():
            take_pair(from_r - 1, c)

        @pl.when(from_l >= 0)
        def _():
            take_pair(from_l, c)

        @pl.when((from_r < line) & (from_l < 0))
        def _():
            take_pair(from_r, c)

    st_copy = remote(stat, stat_in, st_sems.at[0], st_sems.at[1], mate)
    st_copy.start()
    st_copy.wait_recv()
    m_loc = stat[0:1, :]
    m_in = stat_in[0:1, :]
    peak = jnp.maximum(m_loc, m_in)
    total = stat[1:2, :] * jnp.exp(m_loc - peak) + stat_in[1:2, :] * jnp.exp(m_in - peak)
    inv_total = 1.0 / total

    def make_w(slot):
        pos = per_lane(block_of(slot), 0, 1) > 0
        for c in range(CUT):
            part = slot * CUT + c
            scale = jnp.exp(mrec[part][0:1, :] - peak) * inv_total
            target = jnp.where(jnp.logical_and(ahead == c * half, pos), 1.0, 0.0)
            w = (ebuf[part] * scale - target).astype(jnp.bfloat16)
            wbuf[pl.ds(slot * rows + c * half, half)] = w
        return wbuf[pl.ds(slot * rows, rows)]

    def p_grad(slot):
        return dot(make_w(slot), qcat[...], NN) * inv_temp

    def c_copy(d):
        return remote(psend.at[d], chip_in.at[d], c_send.at[d], c_recv.at[d], core)

    def cut(ref, d, c):
        return ref.at[d, pl.ds(c * half, half)]

    def r_copy(d, c):
        i = d * CUT + c
        return remote(cut(zsend, d, c), cut(zin_r, d, c), r_send.at[i], r_recv.at[i], right)

    def l_copy(d, c):
        i = d * CUT + c
        return remote(cut(zsend, d, c), cut(zin_l, d, c), l_send.at[i], l_recv.at[i], left)

    def give(d):
        psend[d] = p_grad(d * 2 + 1 - k).astype(jnp.bfloat16)
        c_copy(d).start()

    def take(d):
        own[d] = p_grad(d * 2 + k)
        c_copy(d).wait_recv()
        own[d] = own[d] + chip_in[d].astype(jnp.float32)

    @pl.loop(0, line - 1)
    def _(s):
        dr = line - 1 - s
        dl = s

        @pl.when(dr > z)
        def _():
            give(dr)

        @pl.when(dl < z)
        def _():
            give(dl)

        @pl.when(dr > z)
        def _():
            take(dr)

            @pl.when(z == 0)
            def _():
                zsend[dr] = own[dr].astype(jnp.bfloat16)
                for c in range(CUT):
                    r_copy(dr, c).start()

        @pl.when(dl < z)
        def _():
            take(dl)

            @pl.when(z == line - 1)
            def _():
                zsend[dl] = own[dl].astype(jnp.bfloat16)
                for c in range(CUT):
                    l_copy(dl, c).start()

    give(z)
    take(z)

    def q_part(start):
        return dot(wbuf[:, pl.ds(start, rows)], pcol[...], TN) * inv_temp

    def pass_on(t):
        n = jnp.maximum(t - z, 0)
        dr = line - 1 - n // CUT
        cr = lax.rem(n, CUT)

        @pl.when((t >= z) & (dr > z) & has_l)
        def _():
            r_copy(dr, cr).wait_recv()
            here = pl.ds(cr * half, half)
            zsend[dr, here] = (own[dr, here] + zin_r[dr, here].astype(jnp.float32)).astype(jnp.bfloat16)
            r_copy(dr, cr).start()

        n = jnp.maximum(t - (line - 1 - z), 0)
        dl = n // CUT
        cl = lax.rem(n, CUT)

        @pl.when((t >= line - 1 - z) & (dl < z) & has_r)
        def _():
            l_copy(dl, cl).wait_recv()
            here = pl.ds(cl * half, half)
            zsend[dl, here] = (own[dl, here] + zin_l[dl, here].astype(jnp.float32)).astype(jnp.bfloat16)
            l_copy(dl, cl).start()

    last = (line - 2) * CUT
    if last >= 1:
        pass_on(1)

    @pl.when(x == 0)
    def _():
        qsend[...] = q_part(rows).astype(jnp.bfloat16)

    @pl.when(x == 1)
    def _():
        qsend[...] = q_part(0).astype(jnp.bfloat16)

    g_copy = remote(qsend, qrecv, g_sems.at[0], g_sems.at[1], mate)
    g_copy.start()

    own_lane = (lane >= x * rows) & (lane < x * rows + rows)
    diag = stat[3:4, :]
    loss = jnp.where(own_lane, peak + jnp.log(total), 0.0) - diag
    grad = stat[2:3, :] * (jnp.exp(m_loc - peak) * inv_total) - diag
    loss = jnp.sum(loss, axis=1, keepdims=True)
    grad = jnp.sum(grad, axis=1, keepdims=True) / inv_temp
    tile_row = lax.broadcasted_iota(jnp.int32, (8, 128), 0)
    acc[0] = jnp.where(tile_row == 0, loss, grad)
    a_copies = []

    def add_up(i):
        copy = remote(acc.at[i], acc_in.at[i], a_send.at[i], a_recv.at[i], pairs[i])
        copy.start()
        copy.wait_recv()
        acc[i + 1] = acc[i] + acc_in[i]
        a_copies.append(copy)

    add_up(0)
    if last >= 2:
        pass_on(2)

    @pl.when(x == 0)
    def _():
        qg_out[...] = q_part(0).astype(jnp.bfloat16)

    @pl.when(x == 1)
    def _():
        qg_out[...] = q_part(rows).astype(jnp.bfloat16)

    add_up(1)

    @pl.loop(3, last + 1)
    def _(t):
        pass_on(t)

    for i in range(2, len(pairs)):
        add_up(i)
    tot_out[...] = acc[len(pairs)]

    g_copy.wait_recv()
    qg_out[...] = (qg_out[...].astype(jnp.float32) + qrecv[...].astype(jnp.float32)).astype(jnp.bfloat16)

    for c in range(CUT):
        here = pl.ds(c * half, half)

        @pl.when(has_l)
        def _(c=c, here=here):
            r_copy(z, c).wait_recv()
            own[z, here] = own[z, here] + zin_r[z, here].astype(jnp.float32)

        @pl.when(has_r)
        def _(c=c, here=here):
            l_copy(z, c).wait_recv()
            own[z, here] = own[z, here] + zin_l[z, here].astype(jnp.float32)

        pg_out[here] = own[z, here].astype(jnp.bfloat16)

    q_copy.wait_send()
    st_copy.wait_send()
    g_copy.wait_send()
    for copy in a_copies:
        copy.wait_send()

    @pl.loop(0, line)
    def _(d):
        c_copy(d).wait_send()
        for c in range(CUT):
            p_copy(d, c, p_core, core).wait_send()

            @pl.when((d <= z) & has_r)
            def _(c=c):
                p_copy(d, c, p_right, right).wait_send()

            @pl.when((d >= z) & has_l)
            def _(c=c):
                p_copy(d, c, p_left, left).wait_send()

            @pl.when(d > z)
            def _(c=c):
                r_copy(d, c).wait_send()

            @pl.when(d < z)
            def _(c=c):
                l_copy(d, c).wait_send()


def fused(line, groups, queries, passages, block_lists, inv_temp):
    rows, width = passages.shape
    stages = 2 + (line.bit_length() - 1) + (groups.bit_length() - 1)
    bf, f32 = jnp.bfloat16, jnp.float32
    block = (rows, width)
    vm, dma = pltpu.VMEM, pltpu.SemaphoreType.DMA
    scratch = [
        vm((2 * line * rows, width), bf),
        vm((2 * rows, width), bf),
        vm((2 * line * CUT, rows // CUT, 2 * rows), f32),
        vm((2 * line * rows, 2 * rows), bf),
        vm((2 * line * CUT, 8, 2 * rows), f32),
        vm((8, 2 * rows), f32),
        vm((8, 2 * rows), f32),
        vm((line,) + block, bf),
        vm((line,) + block, f32),
        vm((line,) + block, bf),
        vm((line,) + block, bf),
        vm((line,) + block, bf),
        vm((line,) + block, bf),
        vm(block, bf),
        vm(block, bf),
        vm((stages + 1, 8, 128), f32),
        vm((stages, 8, 128), f32),
        dma((2,)), dma((2,)), dma((2 * line * CUT,)), dma((line * CUT,)), dma((line * CUT,)),
        dma((line * CUT,)), dma((2,)), dma((line,)), dma((line,)), dma((line * CUT,)),
        dma((line * CUT,)), dma((line * CUT,)), dma((line * CUT,)),
        dma((2,)), dma((stages,)), dma((stages,)),
    ]
    query_grad, passage_grad, totals = pl.pallas_call(
        functools.partial(kernel, line, groups),
        out_shape=(
            jax.ShapeDtypeStruct(block, bf),
            jax.ShapeDtypeStruct(block, bf),
            jax.ShapeDtypeStruct((8, 128), f32),
        ),
        in_specs=[
            pl.BlockSpec(memory_space=pl.ANY),
            pl.BlockSpec(memory_space=pl.ANY),
            pl.BlockSpec(memory_space=pltpu.SMEM),
            pl.BlockSpec(memory_space=pltpu.SMEM),
        ],
        out_specs=(pl.BlockSpec(memory_space=pltpu.VMEM),) * 3,
        scratch_shapes=scratch,
        compiler_params=pltpu.CompilerParams(
            collective_id=0, has_side_effects=True, vmem_limit_bytes=56 * 1024 * 1024
        ),
    )(queries, passages, block_lists, inv_temp.reshape(1))
    pair_count = rows * groups * line * 4
    return query_grad, passage_grad, totals[0, 0] / pair_count, totals[1, 0] / pair_count


def plain(queries, passages, block_lists, inv_temp):
    shard_count = lax.axis_size("shard")
    row_count, feat_width = passages.shape
    listed = block_lists.shape[1]
    col_piece = feat_width // shard_count
    outgoing = passages.reshape(row_count, shard_count, col_piece).transpose(1, 0, 2)
    stripes = lax.all_to_all(outgoing, "shard", split_axis=0, concat_axis=0, tiled=True)
    requests = stripes[block_lists]
    fetched = lax.all_to_all(requests, "shard", split_axis=0, concat_axis=3, tiled=True)
    key_rows = fetched[0]
    logits = inv_temp * jnp.einsum(
        "qd,mkd->mqk", queries, key_rows, preferred_element_type=jnp.float32
    )
    row_peak = jnp.max(logits, axis=(0, 2))
    exp_terms = jnp.exp(logits - row_peak[None, :, None])
    exp_total = jnp.sum(exp_terms, axis=(0, 2))
    row_loss = row_peak + jnp.log(exp_total) - jnp.diagonal(logits[0])
    first_block = (jnp.arange(listed, dtype=jnp.int32) == 0).astype(jnp.float32)
    target = first_block[:, None, None] * jnp.eye(row_count, dtype=jnp.float32)[None]
    residual = exp_terms / exp_total[None, :, None] - target
    weights = residual.astype(jnp.bfloat16)
    temp_part = jnp.sum(residual * logits) / inv_temp
    block_grad = (
        inv_temp * jnp.einsum("mqk,qd->mkd", weights, queries, preferred_element_type=jnp.float32)
    ).astype(jnp.bfloat16)[None]
    query_grad = (
        inv_temp * jnp.einsum("mqk,mkd->qd", weights, key_rows, preferred_element_type=jnp.float32)
    ).astype(jnp.bfloat16)
    block_index = jnp.arange(shard_count, dtype=jnp.int32)
    onehot = (block_lists.reshape(-1)[None, :] == block_index[:, None]).astype(jnp.bfloat16)
    returned = lax.all_to_all(block_grad, "shard", split_axis=3, concat_axis=0, tiled=True)
    summed = jnp.dot(
        onehot,
        returned.reshape(shard_count * listed, row_count * col_piece),
        preferred_element_type=jnp.float32,
    )
    settled = summed.astype(jnp.bfloat16).reshape(shard_count, row_count, col_piece)
    arrived = lax.all_to_all(settled, "shard", split_axis=0, concat_axis=0, tiled=True)
    passage_grad = arrived.transpose(1, 0, 2).reshape(row_count, feat_width)
    totals = lax.psum((jnp.sum(row_loss), temp_part), ("dp", "shard"))
    pair_count = row_count * lax.axis_size("dp") * shard_count
    return query_grad, passage_grad, totals[0] / pair_count, totals[1] / pair_count


def solution(mesh):
    shard_count, groups = mesh.shape["shard"], mesh.shape["dp"]
    line = shard_count // 4
    short = shard_count % 4 == 0 and 2 <= line <= 4 and line & (line - 1) == 0
    body = functools.partial(fused, line, groups) if short and groups & (groups - 1) == 0 else plain
    placed = (P(("dp", "shard"), None), P(("dp", "shard"), None), P("dp", None), P())
    return jax.shard_map(
        body,
        mesh=mesh,
        in_specs=placed,
        out_specs=(P(("dp", "shard"), None), P(("dp", "shard"), None), P(), P()),
        check_vma=False,
    )
```

```python
import functools

import jax
import jax.numpy as jnp
from jax import lax
from jax.experimental import pallas as pl
from jax.experimental.pallas import tpu as pltpu
from jax.sharding import PartitionSpec as P

MESH = pl.DeviceIdType.MESH
LOW = -1e30
NT = (((1,), (1,)), ((), ()))
TN = (((0,), (0,)), ((), ()))
NN = (((1,), (0,)), ((), ()))
CUT = 2


def dot(a, b, dims):
    return lax.dot_general(a, b, dims, preferred_element_type=jnp.float32)


def kernel(line, groups, q_in, p_in, lists, temp, qg_out, pg_out, tot_out,
           pcol, qcat, ebuf, wbuf, mrec, stat, stat_in, chip_in, own, zin_r, zin_l,
           zsend, psend, qsend, qrecv, acc, acc_in,
           loc_sem, q_sems, p_recv, p_right, p_left, p_core, st_sems,
           c_send, c_recv, r_send, r_recv, l_send, l_recv, g_sems, a_send, a_recv):
    rows = q_in.shape[0]
    listed = lists.shape[1]
    half = rows // CUT
    dp = lax.axis_index("dp")
    me = lax.axis_index("shard")
    k = lax.rem(me, 2)
    x = lax.rem(me // 2, 2)
    z = me // 4

    def dev(zz, xx, kk):
        return (dp, (zz * 2 + xx) * 2 + kk)

    core = dev(z, x, 1 - k)
    mate = dev(z, 1 - x, k)
    right = dev(lax.rem(z + 1, line), x, k)
    left = dev(lax.rem(z + line - 1, line), x, k)
    has_r = z < line - 1
    has_l = z > 0
    pairs = [core, mate]
    bit = 1
    far = []
    while bit < line:
        other = z + bit - 2 * bit * lax.rem(z // bit, 2)
        pairs.append(dev(other, x, k))
        if bit > 1:
            far.append(dev(other, x, k))
        bit *= 2
    bit = 1
    while bit < groups:
        other = dp + bit - 2 * bit * lax.rem(dp // bit, 2)
        pairs.append((other, me))
        far.append((other, me))
        bit *= 2

    mine = z * 2 + k
    own_p = pltpu.make_async_copy(p_in, pcol.at[pl.ds(mine * rows, rows)], loc_sem.at[0])
    own_q = pltpu.make_async_copy(q_in, qcat.at[pl.ds(x * rows, rows)], loc_sem.at[1])
    own_p.start()
    own_q.start()

    barrier = pltpu.get_barrier_semaphore()
    for d in [core, mate] + far:
        pl.semaphore_signal(barrier, inc=1, device_id=d, device_id_type=MESH)

    @pl.when(has_r)
    def _():
        pl.semaphore_signal(barrier, inc=1, device_id=right, device_id_type=MESH)

    @pl.when(has_l)
    def _():
        pl.semaphore_signal(barrier, inc=1, device_id=left, device_id_type=MESH)

    ends = jnp.where(has_r, 1, 0) + jnp.where(has_l, 1, 0)
    pl.semaphore_wait(barrier, 2 + len(far) + ends)

    def remote(src, dst, send, recv, d):
        return pltpu.make_async_remote_copy(
            src_ref=src, dst_ref=dst, send_sem=send, recv_sem=recv,
            device_id=d, device_id_type=MESH)

    def p_span(slot, c):
        return pcol.at[pl.ds(slot * rows + c * half, half)]

    def p_copy(zz, c, sems, d):
        slot = zz * 2 + k
        span = p_span(slot, c)
        return remote(span, span, sems.at[zz * CUT + c], p_recv.at[slot * CUT + c], d)

    def p_wait(slot, c):
        span = p_span(slot, c)
        remote(span, span, p_core.at[0], p_recv.at[slot * CUT + c], core).wait_recv()

    my_rows = pl.ds(x * rows, rows)
    q_copy = remote(qcat.at[my_rows], qcat.at[my_rows], q_sems.at[0], q_sems.at[1], mate)
    mate_rows = pl.ds((1 - x) * rows, rows)
    q_wait = remote(qcat.at[mate_rows], qcat.at[mate_rows], q_sems.at[0], q_sems.at[1], mate)

    own_p.wait()

    for c in range(CUT):
        @pl.when(has_r)
        def _(c=c):
            p_copy(z, c, p_right, right).start()

        @pl.when(has_l)
        def _(c=c):
            p_copy(z, c, p_left, left).start()

    own_q.wait()
    q_copy.start()
    for c in range(CUT):
        p_copy(z, c, p_core, core).start()

    lane = lax.broadcasted_iota(jnp.int32, (1, 2 * rows), 1)
    jj = lax.broadcasted_iota(jnp.int32, (half, 2 * rows), 0)
    ii = lax.broadcasted_iota(jnp.int32, (half, 2 * rows), 1)
    ahead = jnp.where(ii < rows, ii, ii - rows) - jj
    inv_temp = temp[0]
    row_a = z * 4 + k
    row_b = z * 4 + 2 + k

    def per_lane(block_id, first, last):
        a = jnp.int32(0)
        b = jnp.int32(0)
        for m in range(first, last):
            a = a + jnp.where(lists[row_a, m] == block_id, 1, 0)
            b = b + jnp.where(lists[row_b, m] == block_id, 1, 0)
        return jnp.where(lane < rows, a, b)

    def block_of(slot):
        return (slot // 2) * 4 + x * 2 + lax.rem(slot, 2)

    stat[0:1, :] = jnp.full((1, 2 * rows), LOW, jnp.float32)
    stat[1:8, :] = jnp.zeros((7, 2 * rows), jnp.float32)

    def consume(slot, c):
        part = slot * CUT + c
        ident = block_of(slot)
        live = per_lane(ident, 0, listed) > 0
        pos = per_lane(ident, 0, 1) > 0
        s = dot(pcol[pl.ds(slot * rows + c * half, half)], qcat[...], NT) * inv_temp
        s = jnp.where(live, s, LOW)
        m_old = stat[0:1, :]
        m_new = jnp.maximum(m_old, jnp.max(s, axis=0, keepdims=True))
        e = jnp.exp(s - m_new)
        ebuf[part] = e
        scale = jnp.exp(m_old - m_new)
        stat[0:1, :] = m_new
        stat[1:2, :] = stat[1:2, :] * scale + jnp.sum(e, axis=0, keepdims=True)
        stat[2:3, :] = stat[2:3, :] * scale + jnp.sum(e * s, axis=0, keepdims=True)
        diag = jnp.sum(jnp.where(ahead == c * half, s, 0.0), axis=0, keepdims=True)
        stat[3:4, :] = stat[3:4, :] + jnp.where(pos, diag, 0.0)
        mrec[part] = jnp.broadcast_to(m_new, (8, 2 * rows))

    def take_pair(zz, c):
        consume(zz * 2 + k, c)
        p_wait(zz * 2 + 1 - k, c)
        consume(zz * 2 + 1 - k, c)

    q_wait.wait_recv()

    @pl.loop(0, (line - 1) * CUT)
    def _(t):
        s = t // CUT
        c = lax.rem(t, CUT)
        from_l = z - 1 - s
        from_r = z + 1 + s

        @pl.when(from_l >= 0)
        def _():
            p_wait(from_l * 2 + k, c)

            @pl.when(has_r)
            def _():
                p_copy(from_l, c, p_right, right).start()

            p_copy(from_l, c, p_core, core).start()

        @pl.when(from_r < line)
        def _():
            p_wait(from_r * 2 + k, c)

            @pl.when(has_l)
            def _():
                p_copy(from_r, c, p_left, left).start()

            p_copy(from_r, c, p_core, core).start()

        @pl.when(s == 0)
        def _():
            take_pair(z, c)

        @pl.when((s > 0) & (from_l + 1 >= 0) & (from_r - 1 < line))
        def _():
            take_pair(from_r - 1, c)

        @pl.when(from_l >= 0)
        def _():
            take_pair(from_l, c)

        @pl.when((from_r < line) & (from_l < 0))
        def _():
            take_pair(from_r, c)

    st_copy = remote(stat, stat_in, st_sems.at[0], st_sems.at[1], mate)
    st_copy.start()
    st_copy.wait_recv()
    m_loc = stat[0:1, :]
    m_in = stat_in[0:1, :]
    peak = jnp.maximum(m_loc, m_in)
    total = stat[1:2, :] * jnp.exp(m_loc - peak) + stat_in[1:2, :] * jnp.exp(m_in - peak)
    inv_total = 1.0 / total

    def make_w(slot):
        pos = per_lane(block_of(slot), 0, 1) > 0
        for c in range(CUT):
            part = slot * CUT + c
            scale = jnp.exp(mrec[part][0:1, :] - peak) * inv_total
            target = jnp.where(jnp.logical_and(ahead == c * half, pos), 1.0, 0.0)
            w = (ebuf[part] * scale - target).astype(jnp.bfloat16)
            wbuf[pl.ds(slot * rows + c * half, half)] = w
        return wbuf[pl.ds(slot * rows, rows)]

    def p_grad(slot):
        return dot(make_w(slot), qcat[...], NN) * inv_temp

    def c_copy(d):
        return remote(psend.at[d], chip_in.at[d], c_send.at[d], c_recv.at[d], core)

    def cut(ref, d, c):
        return ref.at[d, pl.ds(c * half, half)]

    def r_copy(d, c):
        i = d * CUT + c
        return remote(cut(zsend, d, c), cut(zin_r, d, c), r_send.at[i], r_recv.at[i], right)

    def l_copy(d, c):
        i = d * CUT + c
        return remote(cut(zsend, d, c), cut(zin_l, d, c), l_send.at[i], l_recv.at[i], left)

    def give(d):
        psend[d] = p_grad(d * 2 + 1 - k).astype(jnp.bfloat16)
        c_copy(d).start()

    def take(d):
        own[d] = p_grad(d * 2 + k)
        c_copy(d).wait_recv()
        own[d] = own[d] + chip_in[d].astype(jnp.float32)

    @pl.loop(0, line - 1)
    def _(s):
        dr = line - 1 - s
        dl = s

        @pl.when(dr > z)
        def _():
            give(dr)

        @pl.when(dl < z)
        def _():
            give(dl)

        @pl.when(dr > z)
        def _():
            take(dr)

            @pl.when(z == 0)
            def _():
                zsend[dr] = own[dr].astype(jnp.bfloat16)

                @pl.when(s == 0)
                def _():
                    for c in range(CUT):
                        r_copy(dr, c).start()

        @pl.when(dl < z)
        def _():
            take(dl)

            @pl.when(z == line - 1)
            def _():
                zsend[dl] = own[dl].astype(jnp.bfloat16)

                @pl.when(s == 0)
                def _():
                    for c in range(CUT):
                        l_copy(dl, c).start()

    give(z)
    take(z)

    def q_part(start):
        return dot(wbuf[:, pl.ds(start, rows)], pcol[...], TN) * inv_temp

    def pass_on(t):
        n = t - 1
        ahead_of = n // CUT
        cn = lax.rem(n, CUT)

        @pl.when(z == 0)
        def _():
            r_copy(line - 1 - ahead_of, cn).wait_send()
            r_copy(line - 2 - ahead_of, cn).start()

        @pl.when(z == line - 1)
        def _():
            l_copy(ahead_of, cn).wait_send()
            l_copy(ahead_of + 1, cn).start()

        n = jnp.maximum(t - z, 0)
        dr = line - 1 - n // CUT
        cr = lax.rem(n, CUT)

        @pl.when((t >= z) & (dr > z) & has_l)
        def _():
            r_copy(dr, cr).wait_recv()
            here = pl.ds(cr * half, half)
            zsend[dr, here] = (own[dr, here] + zin_r[dr, here].astype(jnp.float32)).astype(jnp.bfloat16)
            r_copy(dr, cr).start()

        n = jnp.maximum(t - (line - 1 - z), 0)
        dl = n // CUT
        cl = lax.rem(n, CUT)

        @pl.when((t >= line - 1 - z) & (dl < z) & has_r)
        def _():
            l_copy(dl, cl).wait_recv()
            here = pl.ds(cl * half, half)
            zsend[dl, here] = (own[dl, here] + zin_l[dl, here].astype(jnp.float32)).astype(jnp.bfloat16)
            l_copy(dl, cl).start()

    last = (line - 2) * CUT
    if last >= 1:
        pass_on(1)

    @pl.when(x == 0)
    def _():
        qsend[...] = q_part(rows).astype(jnp.bfloat16)

    @pl.when(x == 1)
    def _():
        qsend[...] = q_part(0).astype(jnp.bfloat16)

    g_copy = remote(qsend, qrecv, g_sems.at[0], g_sems.at[1], mate)
    g_copy.start()

    own_lane = (lane >= x * rows) & (lane < x * rows + rows)
    diag = stat[3:4, :]
    loss = jnp.where(own_lane, peak + jnp.log(total), 0.0) - diag
    grad = stat[2:3, :] * (jnp.exp(m_loc - peak) * inv_total) - diag
    loss = jnp.sum(loss, axis=1, keepdims=True)
    grad = jnp.sum(grad, axis=1, keepdims=True) / inv_temp
    tile_row = lax.broadcasted_iota(jnp.int32, (8, 128), 0)
    acc[0] = jnp.where(tile_row == 0, loss, grad)
    a_copies = []

    def add_up(i):
        copy = remote(acc.at[i], acc_in.at[i], a_send.at[i], a_recv.at[i], pairs[i])
        copy.start()
        copy.wait_recv()
        acc[i + 1] = acc[i] + acc_in[i]
        a_copies.append(copy)

    add_up(0)
    if last >= 2:
        pass_on(2)

    @pl.when(x == 0)
    def _():
        qg_out[...] = q_part(0).astype(jnp.bfloat16)

    @pl.when(x == 1)
    def _():
        qg_out[...] = q_part(rows).astype(jnp.bfloat16)

    add_up(1)

    @pl.loop(3, last + 1)
    def _(t):
        pass_on(t)

    for i in range(2, len(pairs)):
        add_up(i)
    tot_out[...] = acc[len(pairs)]

    g_copy.wait_recv()
    qg_out[...] = (qg_out[...].astype(jnp.float32) + qrecv[...].astype(jnp.float32)).astype(jnp.bfloat16)

    for c in range(CUT):
        here = pl.ds(c * half, half)

        @pl.when(has_l)
        def _(c=c, here=here):
            r_copy(z, c).wait_recv()
            own[z, here] = own[z, here] + zin_r[z, here].astype(jnp.float32)

        @pl.when(has_r)
        def _(c=c, here=here):
            l_copy(z, c).wait_recv()
            own[z, here] = own[z, here] + zin_l[z, here].astype(jnp.float32)

        pg_out[here] = own[z, here].astype(jnp.bfloat16)

    q_copy.wait_send()
    st_copy.wait_send()
    g_copy.wait_send()
    for copy in a_copies:
        copy.wait_send()

    @pl.loop(0, line)
    def _(d):
        c_copy(d).wait_send()
        for c in range(CUT):
            p_copy(d, c, p_core, core).wait_send()

            @pl.when((d <= z) & has_r)
            def _(c=c):
                p_copy(d, c, p_right, right).wait_send()

            @pl.when((d >= z) & has_l)
            def _(c=c):
                p_copy(d, c, p_left, left).wait_send()

            @pl.when((d > z) & (has_l | (d == 1)))
            def _(c=c):
                r_copy(d, c).wait_send()

            @pl.when((d < z) & (has_r | (d == line - 2)))
            def _(c=c):
                l_copy(d, c).wait_send()


def fused(line, groups, queries, passages, block_lists, inv_temp):
    rows, width = passages.shape
    stages = 2 + (line.bit_length() - 1) + (groups.bit_length() - 1)
    bf, f32 = jnp.bfloat16, jnp.float32
    block = (rows, width)
    vm, dma = pltpu.VMEM, pltpu.SemaphoreType.DMA
    scratch = [
        vm((2 * line * rows, width), bf),
        vm((2 * rows, width), bf),
        vm((2 * line * CUT, rows // CUT, 2 * rows), f32),
        vm((2 * line * rows, 2 * rows), bf),
        vm((2 * line * CUT, 8, 2 * rows), f32),
        vm((8, 2 * rows), f32),
        vm((8, 2 * rows), f32),
        vm((line,) + block, bf),
        vm((line,) + block, f32),
        vm((line,) + block, bf),
        vm((line,) + block, bf),
        vm((line,) + block, bf),
        vm((line,) + block, bf),
        vm(block, bf),
        vm(block, bf),
        vm((stages + 1, 8, 128), f32),
        vm((stages, 8, 128), f32),
        dma((2,)), dma((2,)), dma((2 * line * CUT,)), dma((line * CUT,)), dma((line * CUT,)),
        dma((line * CUT,)), dma((2,)), dma((line,)), dma((line,)), dma((line * CUT,)),
        dma((line * CUT,)), dma((line * CUT,)), dma((line * CUT,)),
        dma((2,)), dma((stages,)), dma((stages,)),
    ]
    query_grad, passage_grad, totals = pl.pallas_call(
        functools.partial(kernel, line, groups),
        out_shape=(
            jax.ShapeDtypeStruct(block, bf),
            jax.ShapeDtypeStruct(block, bf),
            jax.ShapeDtypeStruct((8, 128), f32),
        ),
        in_specs=[
            pl.BlockSpec(memory_space=pl.ANY),
            pl.BlockSpec(memory_space=pl.ANY),
            pl.BlockSpec(memory_space=pltpu.SMEM),
            pl.BlockSpec(memory_space=pltpu.SMEM),
        ],
        out_specs=(pl.BlockSpec(memory_space=pltpu.VMEM),) * 3,
        scratch_shapes=scratch,
        compiler_params=pltpu.CompilerParams(
            collective_id=0, has_side_effects=True, vmem_limit_bytes=56 * 1024 * 1024
        ),
    )(queries, passages, block_lists, inv_temp.reshape(1))
    pair_count = rows * groups * line * 4
    return query_grad, passage_grad, totals[0, 0] / pair_count, totals[1, 0] / pair_count


def plain(queries, passages, block_lists, inv_temp):
    shard_count = lax.axis_size("shard")
    row_count, feat_width = passages.shape
    listed = block_lists.shape[1]
    col_piece = feat_width // shard_count
    outgoing = passages.reshape(row_count, shard_count, col_piece).transpose(1, 0, 2)
    stripes = lax.all_to_all(outgoing, "shard", split_axis=0, concat_axis=0, tiled=True)
    requests = stripes[block_lists]
    fetched = lax.all_to_all(requests, "shard", split_axis=0, concat_axis=3, tiled=True)
    key_rows = fetched[0]
    logits = inv_temp * jnp.einsum(
        "qd,mkd->mqk", queries, key_rows, preferred_element_type=jnp.float32
    )
    row_peak = jnp.max(logits, axis=(0, 2))
    exp_terms = jnp.exp(logits - row_peak[None, :, None])
    exp_total = jnp.sum(exp_terms, axis=(0, 2))
    row_loss = row_peak + jnp.log(exp_total) - jnp.diagonal(logits[0])
    first_block = (jnp.arange(listed, dtype=jnp.int32) == 0).astype(jnp.float32)
    target = first_block[:, None, None] * jnp.eye(row_count, dtype=jnp.float32)[None]
    residual = exp_terms / exp_total[None, :, None] - target
    weights = residual.astype(jnp.bfloat16)
    temp_part = jnp.sum(residual * logits) / inv_temp
    block_grad = (
        inv_temp * jnp.einsum("mqk,qd->mkd", weights, queries, preferred_element_type=jnp.float32)
    ).astype(jnp.bfloat16)[None]
    query_grad = (
        inv_temp * jnp.einsum("mqk,mkd->qd", weights, key_rows, preferred_element_type=jnp.float32)
    ).astype(jnp.bfloat16)
    block_index = jnp.arange(shard_count, dtype=jnp.int32)
    onehot = (block_lists.reshape(-1)[None, :] == block_index[:, None]).astype(jnp.bfloat16)
    returned = lax.all_to_all(block_grad, "shard", split_axis=3, concat_axis=0, tiled=True)
    summed = jnp.dot(
        onehot,
        returned.reshape(shard_count * listed, row_count * col_piece),
        preferred_element_type=jnp.float32,
    )
    settled = summed.astype(jnp.bfloat16).reshape(shard_count, row_count, col_piece)
    arrived = lax.all_to_all(settled, "shard", split_axis=0, concat_axis=0, tiled=True)
    passage_grad = arrived.transpose(1, 0, 2).reshape(row_count, feat_width)
    totals = lax.psum((jnp.sum(row_loss), temp_part), ("dp", "shard"))
    pair_count = row_count * lax.axis_size("dp") * shard_count
    return query_grad, passage_grad, totals[0] / pair_count, totals[1] / pair_count


def solution(mesh):
    shard_count, groups = mesh.shape["shard"], mesh.shape["dp"]
    line = shard_count // 4
    short = shard_count % 4 == 0 and 2 <= line <= 4 and line & (line - 1) == 0
    body = functools.partial(fused, line, groups) if short and groups & (groups - 1) == 0 else plain
    placed = (P(("dp", "shard"), None), P(("dp", "shard"), None), P("dp", None), P())
    return jax.shard_map(
        body,
        mesh=mesh,
        in_specs=placed,
        out_specs=(P(("dp", "shard"), None), P(("dp", "shard"), None), P(), P()),
        check_vma=False,
    )
```

```python
import functools

import jax
import jax.numpy as jnp
from jax import lax
from jax.experimental import pallas as pl
from jax.experimental.pallas import tpu as pltpu
from jax.sharding import PartitionSpec as P

MESH = pl.DeviceIdType.MESH
LOW = -1e30
NT = (((1,), (1,)), ((), ()))
TN = (((0,), (0,)), ((), ()))
NN = (((1,), (0,)), ((), ()))
CUT = 2


def dot(a, b, dims):
    return lax.dot_general(a, b, dims, preferred_element_type=jnp.float32)


def kernel(line, groups, q_in, p_in, lists, temp, qg_out, pg_out, tot_out,
           pcol, qcat, qt, ebuf, wbuf, mrec, stat, stat_in, chip_in, own, zin_r, zin_l,
           zsend, psend, qsend, qrecv, acc, acc_in,
           loc_sem, q_sems, p_recv, p_right, p_left, p_core, st_sems,
           c_send, c_recv, r_send, r_recv, l_send, l_recv, g_sems, a_send, a_recv):
    rows = q_in.shape[0]
    listed = lists.shape[1]
    half = rows // CUT
    wide = 2 * half
    dp = lax.axis_index("dp")
    me = lax.axis_index("shard")
    k = lax.rem(me, 2)
    x = lax.rem(me // 2, 2)
    z = me // 4

    def dev(zz, xx, kk):
        return (dp, (zz * 2 + xx) * 2 + kk)

    core = dev(z, x, 1 - k)
    mate = dev(z, 1 - x, k)
    right = dev(lax.rem(z + 1, line), x, k)
    left = dev(lax.rem(z + line - 1, line), x, k)
    has_r = z < line - 1
    has_l = z > 0
    pairs = [core, mate]
    bit = 1
    far = []
    while bit < line:
        other = z + bit - 2 * bit * lax.rem(z // bit, 2)
        pairs.append(dev(other, x, k))
        if bit > 1:
            far.append(dev(other, x, k))
        bit *= 2
    bit = 1
    while bit < groups:
        other = dp + bit - 2 * bit * lax.rem(dp // bit, 2)
        pairs.append((other, me))
        far.append((other, me))
        bit *= 2

    own_p = [
        pltpu.make_async_copy(
            p_in.at[pl.ds(c * half, half)],
            pcol.at[pl.ds(((z * CUT + c) * 2 + k) * half, half)],
            loc_sem.at[c + 1],
        )
        for c in range(CUT)
    ]
    own_q = pltpu.make_async_copy(q_in, qcat.at[pl.ds(x * rows, rows)], loc_sem.at[0])
    for copy in own_p:
        copy.start()
    own_q.start()

    barrier = pltpu.get_barrier_semaphore()
    for d in [core, mate] + far:
        pl.semaphore_signal(barrier, inc=1, device_id=d, device_id_type=MESH)

    @pl.when(has_r)
    def _():
        pl.semaphore_signal(barrier, inc=1, device_id=right, device_id_type=MESH)

    @pl.when(has_l)
    def _():
        pl.semaphore_signal(barrier, inc=1, device_id=left, device_id_type=MESH)

    ends = jnp.where(has_r, 1, 0) + jnp.where(has_l, 1, 0)
    pl.semaphore_wait(barrier, 2 + len(far) + ends)

    def remote(src, dst, send, recv, d):
        return pltpu.make_async_remote_copy(
            src_ref=src, dst_ref=dst, send_sem=send, recv_sem=recv,
            device_id=d, device_id_type=MESH)

    def p_span(zz, c, kk):
        return pcol.at[pl.ds(((zz * CUT + c) * 2 + kk) * half, half)]

    def p_copy(zz, c, sems, d):
        span = p_span(zz, c, k)
        i = zz * CUT + c
        return remote(span, span, sems.at[i], p_recv.at[i * 2 + k], d)

    def p_wait(zz, c, kk):
        span = p_span(zz, c, kk)
        remote(span, span, p_core.at[0], p_recv.at[(zz * CUT + c) * 2 + kk], core).wait_recv()

    my_rows = pl.ds(x * rows, rows)
    q_copy = remote(qcat.at[my_rows], qcat.at[my_rows], q_sems.at[0], q_sems.at[1], mate)
    mate_rows = pl.ds((1 - x) * rows, rows)
    q_wait = remote(qcat.at[mate_rows], qcat.at[mate_rows], q_sems.at[0], q_sems.at[1], mate)

    for copy in own_p:
        copy.wait()

    for c in range(CUT):
        @pl.when(has_r)
        def _(c=c):
            p_copy(z, c, p_right, right).start()

        @pl.when(has_l)
        def _(c=c):
            p_copy(z, c, p_left, left).start()

    own_q.wait()
    q_copy.start()
    for c in range(CUT):
        p_copy(z, c, p_core, core).start()

    def turn(i):
        qt[:, i * rows:(i + 1) * rows] = qcat[i * rows:(i + 1) * rows, :].T

    @pl.when(x == 0)
    def _():
        turn(0)

    @pl.when(x == 1)
    def _():
        turn(1)

    lane = lax.broadcasted_iota(jnp.int32, (1, 2 * rows), 1)
    jj = lax.broadcasted_iota(jnp.int32, (half, 2 * rows), 0)
    ii = lax.broadcasted_iota(jnp.int32, (half, 2 * rows), 1)
    ahead = jnp.where(ii < rows, ii, ii - rows) - jj
    inv_temp = temp[0]
    row_a = z * 4 + k
    row_b = z * 4 + 2 + k

    def per_lane(block_id, first, last):
        a = jnp.int32(0)
        b = jnp.int32(0)
        for m in range(first, last):
            a = a + jnp.where(lists[row_a, m] == block_id, 1, 0)
            b = b + jnp.where(lists[row_b, m] == block_id, 1, 0)
        return jnp.where(lane < rows, a, b)

    def block_of(zz, kk):
        return zz * 4 + x * 2 + kk

    stat[0:1, :] = jnp.full((1, 2 * rows), LOW, jnp.float32)
    stat[1:8, :] = jnp.zeros((7, 2 * rows), jnp.float32)

    def consume(zz, c):
        part = zz * CUT + c
        live0 = per_lane(block_of(zz, 0), 0, listed) > 0
        live1 = per_lane(block_of(zz, 1), 0, listed) > 0
        pos0 = per_lane(block_of(zz, 0), 0, 1)
        pos1 = per_lane(block_of(zz, 1), 0, 1)
        s = dot(pcol[pl.ds(part * wide, wide)], qt[...], NN) * inv_temp
        s0 = jnp.where(live0, s[:half], LOW)
        s1 = jnp.where(live1, s[half:], LOW)
        s = jnp.concatenate([s0, s1], axis=0)
        m_old = stat[0:1, :]
        m_new = jnp.maximum(m_old, jnp.max(s, axis=0, keepdims=True))
        e = jnp.exp(s - m_new)
        ebuf[part] = e
        scale = jnp.exp(m_old - m_new)
        stat[0:1, :] = m_new
        stat[1:2, :] = stat[1:2, :] * scale + jnp.sum(e, axis=0, keepdims=True)
        stat[2:3, :] = stat[2:3, :] * scale + jnp.sum(e * s, axis=0, keepdims=True)
        diag = jnp.where(ahead == c * half, jnp.where(pos0 > 0, s0, s1), 0.0)
        diag = jnp.sum(diag, axis=0, keepdims=True)
        stat[3:4, :] = stat[3:4, :] + jnp.where(pos0 + pos1 > 0, diag, 0.0)
        mrec[part] = jnp.broadcast_to(m_new, (8, 2 * rows))

    def take_pair(zz, c):
        p_wait(zz, c, 1 - k)
        consume(zz, c)

    q_wait.wait_recv()

    @pl.when(x == 0)
    def _():
        turn(1)

    @pl.when(x == 1)
    def _():
        turn(0)

    @pl.loop(0, (line - 1) * CUT)
    def _(t):
        s = t // CUT
        c = lax.rem(t, CUT)
        from_l = z - 1 - s
        from_r = z + 1 + s

        @pl.when(from_l >= 0)
        def _():
            p_wait(from_l, c, k)

            @pl.when(has_r)
            def _():
                p_copy(from_l, c, p_right, right).start()

            p_copy(from_l, c, p_core, core).start()

        @pl.when(from_r < line)
        def _():
            p_wait(from_r, c, k)

            @pl.when(has_l)
            def _():
                p_copy(from_r, c, p_left, left).start()

            p_copy(from_r, c, p_core, core).start()

        @pl.when(s == 0)
        def _():
            take_pair(z, c)

        @pl.when((s > 0) & (from_l + 1 >= 0) & (from_r - 1 < line))
        def _():
            take_pair(from_r - 1, c)

        @pl.when(from_l >= 0)
        def _():
            take_pair(from_l, c)

        @pl.when((from_r < line) & (from_l < 0))
        def _():
            take_pair(from_r, c)

    st_copy = remote(stat, stat_in, st_sems.at[0], st_sems.at[1], mate)
    st_copy.start()
    st_copy.wait_recv()
    m_loc = stat[0:1, :]
    m_in = stat_in[0:1, :]
    peak = jnp.maximum(m_loc, m_in)
    total = stat[1:2, :] * jnp.exp(m_loc - peak) + stat_in[1:2, :] * jnp.exp(m_in - peak)
    inv_total = 1.0 / total

    own_lane = (lane >= x * rows) & (lane < x * rows + rows)
    diag_row = stat[3:4, :]
    loss = jnp.where(own_lane, peak + jnp.log(total), 0.0) - diag_row
    grad = stat[2:3, :] * (jnp.exp(m_loc - peak) * inv_total) - diag_row
    loss = jnp.sum(loss, axis=1, keepdims=True)
    grad = jnp.sum(grad, axis=1, keepdims=True) / inv_temp
    tile_row = lax.broadcasted_iota(jnp.int32, (8, 128), 0)
    acc[0] = jnp.where(tile_row == 0, loss, grad)
    a_copies = [
        remote(acc.at[i], acc_in.at[i], a_send.at[i], a_recv.at[i], d) for i, d in enumerate(pairs)
    ]
    a_copies[0].start()

    def add_up(i):
        a_copies[i].wait_recv()
        acc[i + 1] = acc[i] + acc_in[i]
        if i + 1 < len(pairs):
            a_copies[i + 1].start()

    def p_grad(d):
        pos0 = per_lane(block_of(d, 0), 0, 1) > 0
        pos1 = per_lane(block_of(d, 1), 0, 1) > 0
        for c in range(CUT):
            part = d * CUT + c
            scale = jnp.exp(mrec[part][0:1, :] - peak) * inv_total
            w = ebuf[part] * scale
            w0 = w[:half] - jnp.where(jnp.logical_and(ahead == c * half, pos0), 1.0, 0.0)
            w1 = w[half:] - jnp.where(jnp.logical_and(ahead == c * half, pos1), 1.0, 0.0)
            wbuf[pl.ds(part * wide, half)] = w0.astype(jnp.bfloat16)
            wbuf[pl.ds(part * wide + half, half)] = w1.astype(jnp.bfloat16)
        g = dot(wbuf[pl.ds(d * CUT * wide, CUT * wide)], qcat[...], NN) * inv_temp
        own[d] = g.reshape(2 * CUT, half, q_in.shape[1])

    def c_copy(d):
        return remote(psend.at[d], chip_in.at[d], c_send.at[d], c_recv.at[d], core)

    def r_copy(d, c):
        i = d * CUT + c
        return remote(zsend.at[d, c], zin_r.at[d, c], r_send.at[i], r_recv.at[i], right)

    def l_copy(d, c):
        i = d * CUT + c
        return remote(zsend.at[d, c], zin_l.at[d, c], l_send.at[i], l_recv.at[i], left)

    def give(d):
        p_grad(d)
        for c in range(CUT):
            psend[d, c] = own[d, c * 2 + 1 - k].astype(jnp.bfloat16)
        c_copy(d).start()

    def take(d):
        c_copy(d).wait_recv()
        for c in range(CUT):
            own[d, c * 2 + k] = own[d, c * 2 + k] + chip_in[d, c].astype(jnp.float32)

    for s in range(line - 1):
        dr = line - 1 - s
        dl = s

        @pl.when(dr > z)
        def _(dr=dr):
            give(dr)

        @pl.when(dl < z)
        def _(dl=dl):
            give(dl)

        @pl.when(dr > z)
        def _(s=s, dr=dr):
            take(dr)

            @pl.when(z == 0)
            def _():
                for c in range(CUT):
                    zsend[dr, c] = own[dr, c * 2 + k].astype(jnp.bfloat16)
                    if s == 0:
                        r_copy(dr, c).start()

        @pl.when(dl < z)
        def _(s=s, dl=dl):
            take(dl)

            @pl.when(z == line - 1)
            def _():
                for c in range(CUT):
                    zsend[dl, c] = own[dl, c * 2 + k].astype(jnp.bfloat16)
                    if s == 0:
                        l_copy(dl, c).start()

        if s < 2:
            add_up(s)

    give(z)
    take(z)

    def q_part(start):
        return dot(wbuf[:, pl.ds(start, rows)], pcol[...], TN) * inv_temp

    def pass_on(t):
        n = t - 1
        ahead_of = n // CUT
        cn = lax.rem(n, CUT)

        @pl.when(z == 0)
        def _():
            r_copy(line - 1 - ahead_of, cn).wait_send()
            r_copy(line - 2 - ahead_of, cn).start()

        @pl.when(z == line - 1)
        def _():
            l_copy(ahead_of, cn).wait_send()
            l_copy(ahead_of + 1, cn).start()

        n = jnp.maximum(t - z, 0)
        dr = line - 1 - n // CUT
        cr = lax.rem(n, CUT)

        @pl.when((t >= z) & (dr > z) & has_l)
        def _():
            r_copy(dr, cr).wait_recv()
            zsend[dr, cr] = (own[dr, cr * 2 + k] + zin_r[dr, cr].astype(jnp.float32)).astype(jnp.bfloat16)
            r_copy(dr, cr).start()

        n = jnp.maximum(t - (line - 1 - z), 0)
        dl = n // CUT
        cl = lax.rem(n, CUT)

        @pl.when((t >= line - 1 - z) & (dl < z) & has_r)
        def _():
            l_copy(dl, cl).wait_recv()
            zsend[dl, cl] = (own[dl, cl * 2 + k] + zin_l[dl, cl].astype(jnp.float32)).astype(jnp.bfloat16)
            l_copy(dl, cl).start()

    last = (line - 2) * CUT
    if last >= 1:
        pass_on(1)

    @pl.when(x == 0)
    def _():
        qsend[...] = q_part(rows).astype(jnp.bfloat16)

    @pl.when(x == 1)
    def _():
        qsend[...] = q_part(0).astype(jnp.bfloat16)

    g_copy = remote(qsend, qrecv, g_sems.at[0], g_sems.at[1], mate)
    g_copy.start()

    add_up(min(2, line - 1))
    if last >= 2:
        pass_on(2)

    @pl.when(x == 0)
    def _():
        qg_out[...] = q_part(0).astype(jnp.bfloat16)

    @pl.when(x == 1)
    def _():
        qg_out[...] = q_part(rows).astype(jnp.bfloat16)

    add_up(min(2, line - 1) + 1)

    @pl.loop(3, last + 1)
    def _(t):
        pass_on(t)

    for i in range(min(2, line - 1) + 2, len(pairs)):
        add_up(i)
    tot_out[...] = acc[len(pairs)]

    g_copy.wait_recv()
    qg_out[...] = (qg_out[...].astype(jnp.float32) + qrecv[...].astype(jnp.float32)).astype(jnp.bfloat16)

    for c in range(CUT):
        @pl.when(has_l)
        def _(c=c):
            r_copy(z, c).wait_recv()
            own[z, c * 2 + k] = own[z, c * 2 + k] + zin_r[z, c].astype(jnp.float32)

        @pl.when(has_r)
        def _(c=c):
            l_copy(z, c).wait_recv()
            own[z, c * 2 + k] = own[z, c * 2 + k] + zin_l[z, c].astype(jnp.float32)

        pg_out[pl.ds(c * half, half)] = own[z, c * 2 + k].astype(jnp.bfloat16)

    q_copy.wait_send()
    st_copy.wait_send()
    g_copy.wait_send()
    for copy in a_copies:
        copy.wait_send()

    @pl.loop(0, line)
    def _(d):
        c_copy(d).wait_send()
        for c in range(CUT):
            p_copy(d, c, p_core, core).wait_send()

            @pl.when((d <= z) & has_r)
            def _(c=c):
                p_copy(d, c, p_right, right).wait_send()

            @pl.when((d >= z) & has_l)
            def _(c=c):
                p_copy(d, c, p_left, left).wait_send()

            @pl.when((d > z) & (has_l | (d == 1)))
            def _(c=c):
                r_copy(d, c).wait_send()

            @pl.when((d < z) & (has_r | (d == line - 2)))
            def _(c=c):
                l_copy(d, c).wait_send()


def fused(line, groups, queries, passages, block_lists, inv_temp):
    rows, width = passages.shape
    stages = 2 + (line.bit_length() - 1) + (groups.bit_length() - 1)
    bf, f32 = jnp.bfloat16, jnp.float32
    block = (rows, width)
    half = rows // CUT
    pieces = (CUT, half, width)
    vm, dma = pltpu.VMEM, pltpu.SemaphoreType.DMA
    scratch = [
        vm((2 * line * rows, width), bf),
        vm((2 * rows, width), bf),
        vm((width, 2 * rows), bf),
        vm((line * CUT, 2 * half, 2 * rows), f32),
        vm((2 * line * rows, 2 * rows), bf),
        vm((line * CUT, 8, 2 * rows), f32),
        vm((8, 2 * rows), f32),
        vm((8, 2 * rows), f32),
        vm((line,) + pieces, bf),
        vm((line, 2 * CUT, half, width), f32),
        vm((line,) + pieces, bf),
        vm((line,) + pieces, bf),
        vm((line,) + pieces, bf),
        vm((line,) + pieces, bf),
        vm(block, bf),
        vm(block, bf),
        vm((stages + 1, 8, 128), f32),
        vm((stages, 8, 128), f32),
        dma((CUT + 1,)), dma((2,)), dma((2 * line * CUT,)), dma((line * CUT,)), dma((line * CUT,)),
        dma((line * CUT,)), dma((2,)), dma((line,)), dma((line,)), dma((line * CUT,)),
        dma((line * CUT,)), dma((line * CUT,)), dma((line * CUT,)),
        dma((2,)), dma((stages,)), dma((stages,)),
    ]
    query_grad, passage_grad, totals = pl.pallas_call(
        functools.partial(kernel, line, groups),
        out_shape=(
            jax.ShapeDtypeStruct(block, bf),
            jax.ShapeDtypeStruct(block, bf),
            jax.ShapeDtypeStruct((8, 128), f32),
        ),
        in_specs=[
            pl.BlockSpec(memory_space=pl.ANY),
            pl.BlockSpec(memory_space=pl.ANY),
            pl.BlockSpec(memory_space=pltpu.SMEM),
            pl.BlockSpec(memory_space=pltpu.SMEM),
        ],
        out_specs=(pl.BlockSpec(memory_space=pltpu.VMEM),) * 3,
        scratch_shapes=scratch,
        compiler_params=pltpu.CompilerParams(
            collective_id=0, has_side_effects=True, vmem_limit_bytes=56 * 1024 * 1024
        ),
    )(queries, passages, block_lists, inv_temp.reshape(1))
    pair_count = rows * groups * line * 4
    return query_grad, passage_grad, totals[0, 0] / pair_count, totals[1, 0] / pair_count


def plain(queries, passages, block_lists, inv_temp):
    shard_count = lax.axis_size("shard")
    row_count, feat_width = passages.shape
    listed = block_lists.shape[1]
    col_piece = feat_width // shard_count
    outgoing = passages.reshape(row_count, shard_count, col_piece).transpose(1, 0, 2)
    stripes = lax.all_to_all(outgoing, "shard", split_axis=0, concat_axis=0, tiled=True)
    requests = stripes[block_lists]
    fetched = lax.all_to_all(requests, "shard", split_axis=0, concat_axis=3, tiled=True)
    key_rows = fetched[0]
    logits = inv_temp * jnp.einsum(
        "qd,mkd->mqk", queries, key_rows, preferred_element_type=jnp.float32
    )
    row_peak = jnp.max(logits, axis=(0, 2))
    exp_terms = jnp.exp(logits - row_peak[None, :, None])
    exp_total = jnp.sum(exp_terms, axis=(0, 2))
    row_loss = row_peak + jnp.log(exp_total) - jnp.diagonal(logits[0])
    first_block = (jnp.arange(listed, dtype=jnp.int32) == 0).astype(jnp.float32)
    target = first_block[:, None, None] * jnp.eye(row_count, dtype=jnp.float32)[None]
    residual = exp_terms / exp_total[None, :, None] - target
    weights = residual.astype(jnp.bfloat16)
    temp_part = jnp.sum(residual * logits) / inv_temp
    block_grad = (
        inv_temp * jnp.einsum("mqk,qd->mkd", weights, queries, preferred_element_type=jnp.float32)
    ).astype(jnp.bfloat16)[None]
    query_grad = (
        inv_temp * jnp.einsum("mqk,mkd->qd", weights, key_rows, preferred_element_type=jnp.float32)
    ).astype(jnp.bfloat16)
    block_index = jnp.arange(shard_count, dtype=jnp.int32)
    onehot = (block_lists.reshape(-1)[None, :] == block_index[:, None]).astype(jnp.bfloat16)
    returned = lax.all_to_all(block_grad, "shard", split_axis=3, concat_axis=0, tiled=True)
    summed = jnp.dot(
        onehot,
        returned.reshape(shard_count * listed, row_count * col_piece),
        preferred_element_type=jnp.float32,
    )
    settled = summed.astype(jnp.bfloat16).reshape(shard_count, row_count, col_piece)
    arrived = lax.all_to_all(settled, "shard", split_axis=0, concat_axis=0, tiled=True)
    passage_grad = arrived.transpose(1, 0, 2).reshape(row_count, feat_width)
    totals = lax.psum((jnp.sum(row_loss), temp_part), ("dp", "shard"))
    pair_count = row_count * lax.axis_size("dp") * shard_count
    return query_grad, passage_grad, totals[0] / pair_count, totals[1] / pair_count


def solution(mesh):
    shard_count, groups = mesh.shape["shard"], mesh.shape["dp"]
    line = shard_count // 4
    short = shard_count % 4 == 0 and 2 <= line <= 4 and line & (line - 1) == 0
    body = functools.partial(fused, line, groups) if short and groups & (groups - 1) == 0 else plain
    placed = (P(("dp", "shard"), None), P(("dp", "shard"), None), P("dp", None), P())
    return jax.shard_map(
        body,
        mesh=mesh,
        in_specs=placed,
        out_specs=(P(("dp", "shard"), None), P(("dp", "shard"), None), P(), P()),
        check_vma=False,
    )
```

```python
import functools

import jax
import jax.numpy as jnp
from jax import lax
from jax.experimental import pallas as pl
from jax.experimental.pallas import tpu as pltpu
from jax.sharding import PartitionSpec as P

MESH = pl.DeviceIdType.MESH
LOW = -1e30
NT = (((1,), (1,)), ((), ()))
TN = (((0,), (0,)), ((), ()))
NN = (((1,), (0,)), ((), ()))
CUT = 2


def dot(a, b, dims):
    return lax.dot_general(a, b, dims, preferred_element_type=jnp.float32)


def kernel(line, groups, q_in, p_in, lists, temp, qg_out, pg_out, tot_out,
           pcol, qcat, qt, ebuf, wbuf, mrec, stat, stat_in, chip_in, own, zin_r, zin_l,
           zsend, psend, qsend, qrecv, acc, acc_in,
           loc_sem, q_sems, p_recv, p_right, p_left, p_core, st_sems,
           c_send, c_recv, r_send, r_recv, l_send, l_recv, g_sems, a_send, a_recv):
    rows = q_in.shape[0]
    listed = lists.shape[0]
    half = rows // CUT
    wide = 2 * half
    dp = lax.axis_index("dp")
    me = lax.axis_index("shard")
    k = lax.rem(me, 2)
    x = lax.rem(me // 2, 2)
    z = me // 4

    def dev(zz, xx, kk):
        return (dp, (zz * 2 + xx) * 2 + kk)

    core = dev(z, x, 1 - k)
    mate = dev(z, 1 - x, k)
    right = dev(lax.rem(z + 1, line), x, k)
    left = dev(lax.rem(z + line - 1, line), x, k)
    has_r = z < line - 1
    has_l = z > 0
    pairs = [core, mate]
    bit = 1
    far = []
    while bit < line:
        other = z + bit - 2 * bit * lax.rem(z // bit, 2)
        pairs.append(dev(other, x, k))
        if bit > 1:
            far.append(dev(other, x, k))
        bit *= 2
    bit = 1
    while bit < groups:
        other = dp + bit - 2 * bit * lax.rem(dp // bit, 2)
        pairs.append((other, me))
        far.append((other, me))
        bit *= 2

    own_p = [
        pltpu.make_async_copy(
            p_in.at[pl.ds(c * half, half)],
            pcol.at[pl.ds(((z * CUT + c) * 2 + k) * half, half)],
            loc_sem.at[c + 1],
        )
        for c in range(CUT)
    ]
    own_q = pltpu.make_async_copy(q_in, qcat.at[pl.ds(x * rows, rows)], loc_sem.at[0])
    for copy in own_p:
        copy.start()
    own_q.start()

    barrier = pltpu.get_barrier_semaphore()
    for d in [core, mate] + far:
        pl.semaphore_signal(barrier, inc=1, device_id=d, device_id_type=MESH)

    @pl.when(has_r)
    def _():
        pl.semaphore_signal(barrier, inc=1, device_id=right, device_id_type=MESH)

    @pl.when(has_l)
    def _():
        pl.semaphore_signal(barrier, inc=1, device_id=left, device_id_type=MESH)

    ends = jnp.where(has_r, 1, 0) + jnp.where(has_l, 1, 0)
    pl.semaphore_wait(barrier, 2 + len(far) + ends)

    def remote(src, dst, send, recv, d):
        return pltpu.make_async_remote_copy(
            src_ref=src, dst_ref=dst, send_sem=send, recv_sem=recv,
            device_id=d, device_id_type=MESH)

    def p_span(zz, c, kk):
        return pcol.at[pl.ds(((zz * CUT + c) * 2 + kk) * half, half)]

    def p_copy(zz, c, sems, d):
        span = p_span(zz, c, k)
        i = zz * CUT + c
        return remote(span, span, sems.at[i], p_recv.at[i * 2 + k], d)

    def p_wait(zz, c, kk):
        span = p_span(zz, c, kk)
        remote(span, span, p_core.at[0], p_recv.at[(zz * CUT + c) * 2 + kk], core).wait_recv()

    my_rows = pl.ds(x * rows, rows)
    q_copy = remote(qcat.at[my_rows], qcat.at[my_rows], q_sems.at[0], q_sems.at[1], mate)
    mate_rows = pl.ds((1 - x) * rows, rows)
    q_wait = remote(qcat.at[mate_rows], qcat.at[mate_rows], q_sems.at[0], q_sems.at[1], mate)

    for copy in own_p:
        copy.wait()

    for c in range(CUT):
        @pl.when(has_r)
        def _(c=c):
            p_copy(z, c, p_right, right).start()

        @pl.when(has_l)
        def _(c=c):
            p_copy(z, c, p_left, left).start()

    own_q.wait()
    q_copy.start()
    for c in range(CUT):
        p_copy(z, c, p_core, core).start()

    def turn(i):
        qt[:, i * rows:(i + 1) * rows] = qcat[i * rows:(i + 1) * rows, :].T

    @pl.when(x == 0)
    def _():
        turn(0)

    @pl.when(x == 1)
    def _():
        turn(1)

    lane = lax.broadcasted_iota(jnp.int32, (1, 2 * rows), 1)
    jj = lax.broadcasted_iota(jnp.int32, (half, 2 * rows), 0)
    ii = lax.broadcasted_iota(jnp.int32, (half, 2 * rows), 1)
    ahead = jnp.where(ii < rows, ii, ii - rows) - jj
    inv_temp = temp[0]
    row_a = z * 4 + k
    row_b = z * 4 + 2 + k

    def per_lane(block_id, first, last):
        a = jnp.int32(0)
        b = jnp.int32(0)
        for m in range(first, last):
            a = a + jnp.where(lists[m, row_a] == block_id, 1, 0)
            b = b + jnp.where(lists[m, row_b] == block_id, 1, 0)
        return jnp.where(lane < rows, a, b)

    def block_of(zz, kk):
        return zz * 4 + x * 2 + kk

    stat[0:1, :] = jnp.full((1, 2 * rows), LOW, jnp.float32)
    stat[1:8, :] = jnp.zeros((7, 2 * rows), jnp.float32)

    def consume(zz, c):
        part = zz * CUT + c
        live0 = per_lane(block_of(zz, 0), 0, listed) > 0
        live1 = per_lane(block_of(zz, 1), 0, listed) > 0
        pos0 = per_lane(block_of(zz, 0), 0, 1)
        pos1 = per_lane(block_of(zz, 1), 0, 1)
        s = dot(pcol[pl.ds(part * wide, wide)], qt[...], NN) * inv_temp
        s0 = jnp.where(live0, s[:half], LOW)
        s1 = jnp.where(live1, s[half:], LOW)
        s = jnp.concatenate([s0, s1], axis=0)
        m_old = stat[0:1, :]
        m_new = jnp.maximum(m_old, jnp.max(s, axis=0, keepdims=True))
        e = jnp.exp(s - m_new)
        ebuf[part] = e
        scale = jnp.exp(m_old - m_new)
        stat[0:1, :] = m_new
        stat[1:2, :] = stat[1:2, :] * scale + jnp.sum(e, axis=0, keepdims=True)
        stat[2:3, :] = stat[2:3, :] * scale + jnp.sum(e * s, axis=0, keepdims=True)
        diag = jnp.where(ahead == c * half, jnp.where(pos0 > 0, s0, s1), 0.0)
        diag = jnp.sum(diag, axis=0, keepdims=True)
        stat[3:4, :] = stat[3:4, :] + jnp.where(pos0 + pos1 > 0, diag, 0.0)
        mrec[part] = jnp.broadcast_to(m_new, (8, 2 * rows))

    def take_pair(zz, c):
        p_wait(zz, c, 1 - k)
        consume(zz, c)

    q_wait.wait_recv()

    @pl.when(x == 0)
    def _():
        turn(1)

    @pl.when(x == 1)
    def _():
        turn(0)

    @pl.loop(0, (line - 1) * CUT)
    def _(t):
        s = t // CUT
        c = lax.rem(t, CUT)
        from_l = z - 1 - s
        from_r = z + 1 + s

        @pl.when(from_l >= 0)
        def _():
            p_wait(from_l, c, k)

            @pl.when(has_r)
            def _():
                p_copy(from_l, c, p_right, right).start()

            p_copy(from_l, c, p_core, core).start()

        @pl.when(from_r < line)
        def _():
            p_wait(from_r, c, k)

            @pl.when(has_l)
            def _():
                p_copy(from_r, c, p_left, left).start()

            p_copy(from_r, c, p_core, core).start()

        @pl.when(s == 0)
        def _():
            take_pair(z, c)

        @pl.when((s > 0) & (from_l + 1 >= 0) & (from_r - 1 < line))
        def _():
            take_pair(from_r - 1, c)

        @pl.when(from_l >= 0)
        def _():
            take_pair(from_l, c)

        @pl.when((from_r < line) & (from_l < 0))
        def _():
            take_pair(from_r, c)

    st_copy = remote(stat, stat_in, st_sems.at[0], st_sems.at[1], mate)
    st_copy.start()
    st_copy.wait_recv()
    m_loc = stat[0:1, :]
    m_in = stat_in[0:1, :]
    peak = jnp.maximum(m_loc, m_in)
    total = stat[1:2, :] * jnp.exp(m_loc - peak) + stat_in[1:2, :] * jnp.exp(m_in - peak)
    inv_total = 1.0 / total

    own_lane = (lane >= x * rows) & (lane < x * rows + rows)
    diag_row = stat[3:4, :]
    loss = jnp.where(own_lane, peak + jnp.log(total), 0.0) - diag_row
    grad = stat[2:3, :] * (jnp.exp(m_loc - peak) * inv_total) - diag_row
    loss = jnp.sum(loss, axis=1, keepdims=True)
    grad = jnp.sum(grad, axis=1, keepdims=True) / inv_temp
    tile_row = lax.broadcasted_iota(jnp.int32, (8, 128), 0)
    acc[0] = jnp.where(tile_row == 0, loss, grad)
    a_copies = [
        remote(acc.at[i], acc_in.at[i], a_send.at[i], a_recv.at[i], d) for i, d in enumerate(pairs)
    ]
    a_copies[0].start()

    def add_up(i):
        a_copies[i].wait_recv()
        acc[i + 1] = acc[i] + acc_in[i]
        if i + 1 < len(pairs):
            a_copies[i + 1].start()

    def c_copy(d, c):
        i = d * CUT + c
        return remote(psend.at[d, c], chip_in.at[d, c], c_send.at[i], c_recv.at[i], core)

    def r_copy(d, c):
        i = d * CUT + c
        return remote(zsend.at[d, c], zin_r.at[d, c], r_send.at[i], r_recv.at[i], right)

    def l_copy(d, c):
        i = d * CUT + c
        return remote(zsend.at[d, c], zin_l.at[d, c], l_send.at[i], l_recv.at[i], left)

    def give(d):
        pos0 = per_lane(block_of(d, 0), 0, 1) > 0
        pos1 = per_lane(block_of(d, 1), 0, 1) > 0
        for c in range(CUT):
            part = d * CUT + c
            scale = jnp.exp(mrec[part][0:1, :] - peak) * inv_total
            w = ebuf[part] * scale
            w0 = w[:half] - jnp.where(jnp.logical_and(ahead == c * half, pos0), 1.0, 0.0)
            w1 = w[half:] - jnp.where(jnp.logical_and(ahead == c * half, pos1), 1.0, 0.0)
            wbuf[pl.ds(part * wide, half)] = w0.astype(jnp.bfloat16)
            wbuf[pl.ds(part * wide + half, half)] = w1.astype(jnp.bfloat16)
            g = dot(wbuf[pl.ds(part * wide, wide)], qcat[...], NN) * inv_temp
            own[d, pl.ds(2 * c, 2)] = g.reshape(2, half, q_in.shape[1])
            psend[d, c] = own[d, c * 2 + 1 - k].astype(jnp.bfloat16)
            c_copy(d, c).start()

    def take(d, c):
        c_copy(d, c).wait_recv()
        own[d, c * 2 + k] = own[d, c * 2 + k] + chip_in[d, c].astype(jnp.float32)

    for s in range(line - 1):
        dr = line - 1 - s
        dl = s

        @pl.when(dr > z)
        def _(dr=dr):
            give(dr)

        @pl.when(dl < z)
        def _(dl=dl):
            give(dl)

        @pl.when(dr > z)
        def _(s=s, dr=dr):
            for c in range(CUT):
                take(dr, c)

                @pl.when(z == 0)
                def _(c=c):
                    zsend[dr, c] = own[dr, c * 2 + k].astype(jnp.bfloat16)
                    if s == 0:
                        r_copy(dr, c).start()

        @pl.when(dl < z)
        def _(s=s, dl=dl):
            for c in range(CUT):
                take(dl, c)

                @pl.when(z == line - 1)
                def _(c=c):
                    zsend[dl, c] = own[dl, c * 2 + k].astype(jnp.bfloat16)
                    if s == 0:
                        l_copy(dl, c).start()

        if s < 2:
            add_up(s)

    give(z)
    for c in range(CUT):
        take(z, c)

    def q_part(start):
        return dot(wbuf[:, pl.ds(start, rows)], pcol[...], TN) * inv_temp

    def pass_on(t):
        n = t - 1
        ahead_of = n // CUT
        cn = lax.rem(n, CUT)

        @pl.when(z == 0)
        def _():
            r_copy(line - 1 - ahead_of, cn).wait_send()
            r_copy(line - 2 - ahead_of, cn).start()

        @pl.when(z == line - 1)
        def _():
            l_copy(ahead_of, cn).wait_send()
            l_copy(ahead_of + 1, cn).start()

        n = jnp.maximum(t - z, 0)
        dr = line - 1 - n // CUT
        cr = lax.rem(n, CUT)

        @pl.when((t >= z) & (dr > z) & has_l)
        def _():
            r_copy(dr, cr).wait_recv()
            zsend[dr, cr] = (own[dr, cr * 2 + k] + zin_r[dr, cr].astype(jnp.float32)).astype(jnp.bfloat16)
            r_copy(dr, cr).start()

        n = jnp.maximum(t - (line - 1 - z), 0)
        dl = n // CUT
        cl = lax.rem(n, CUT)

        @pl.when((t >= line - 1 - z) & (dl < z) & has_r)
        def _():
            l_copy(dl, cl).wait_recv()
            zsend[dl, cl] = (own[dl, cl * 2 + k] + zin_l[dl, cl].astype(jnp.float32)).astype(jnp.bfloat16)
            l_copy(dl, cl).start()

    last = (line - 2) * CUT
    if last >= 1:
        pass_on(1)

    @pl.when(x == 0)
    def _():
        qsend[...] = q_part(rows).astype(jnp.bfloat16)

    @pl.when(x == 1)
    def _():
        qsend[...] = q_part(0).astype(jnp.bfloat16)

    g_copy = remote(qsend, qrecv, g_sems.at[0], g_sems.at[1], mate)
    g_copy.start()

    add_up(min(2, line - 1))
    if last >= 2:
        pass_on(2)

    @pl.when(x == 0)
    def _():
        qg_out[...] = q_part(0).astype(jnp.bfloat16)

    @pl.when(x == 1)
    def _():
        qg_out[...] = q_part(rows).astype(jnp.bfloat16)

    add_up(min(2, line - 1) + 1)

    @pl.loop(3, last + 1)
    def _(t):
        pass_on(t)

    for i in range(min(2, line - 1) + 2, len(pairs)):
        add_up(i)
    tot_out[...] = acc[len(pairs)]

    g_copy.wait_recv()
    qg_out[...] = (qg_out[...].astype(jnp.float32) + qrecv[...].astype(jnp.float32)).astype(jnp.bfloat16)

    for c in range(CUT):
        @pl.when(has_l)
        def _(c=c):
            r_copy(z, c).wait_recv()
            own[z, c * 2 + k] = own[z, c * 2 + k] + zin_r[z, c].astype(jnp.float32)

        @pl.when(has_r)
        def _(c=c):
            l_copy(z, c).wait_recv()
            own[z, c * 2 + k] = own[z, c * 2 + k] + zin_l[z, c].astype(jnp.float32)

        pg_out[pl.ds(c * half, half)] = own[z, c * 2 + k].astype(jnp.bfloat16)

    q_copy.wait_send()
    st_copy.wait_send()
    g_copy.wait_send()
    for copy in a_copies:
        copy.wait_send()

    @pl.loop(0, line)
    def _(d):
        for c in range(CUT):
            c_copy(d, c).wait_send()
            p_copy(d, c, p_core, core).wait_send()

            @pl.when((d <= z) & has_r)
            def _(c=c):
                p_copy(d, c, p_right, right).wait_send()

            @pl.when((d >= z) & has_l)
            def _(c=c):
                p_copy(d, c, p_left, left).wait_send()

            @pl.when((d > z) & (has_l | (d == 1)))
            def _(c=c):
                r_copy(d, c).wait_send()

            @pl.when((d < z) & (has_r | (d == line - 2)))
            def _(c=c):
                l_copy(d, c).wait_send()


def fused(line, groups, queries, passages, block_lists, inv_temp):
    rows, width = passages.shape
    stages = 2 + (line.bit_length() - 1) + (groups.bit_length() - 1)
    bf, f32 = jnp.bfloat16, jnp.float32
    block = (rows, width)
    half = rows // CUT
    pieces = (CUT, half, width)
    vm, dma = pltpu.VMEM, pltpu.SemaphoreType.DMA
    scratch = [
        vm((2 * line * rows, width), bf),
        vm((2 * rows, width), bf),
        vm((width, 2 * rows), bf),
        vm((line * CUT, 2 * half, 2 * rows), f32),
        vm((2 * line * rows, 2 * rows), bf),
        vm((line * CUT, 8, 2 * rows), f32),
        vm((8, 2 * rows), f32),
        vm((8, 2 * rows), f32),
        vm((line,) + pieces, bf),
        vm((line, 2 * CUT, half, width), f32),
        vm((line,) + pieces, bf),
        vm((line,) + pieces, bf),
        vm((line,) + pieces, bf),
        vm((line,) + pieces, bf),
        vm(block, bf),
        vm(block, bf),
        vm((stages + 1, 8, 128), f32),
        vm((stages, 8, 128), f32),
        dma((CUT + 1,)), dma((2,)), dma((2 * line * CUT,)), dma((line * CUT,)), dma((line * CUT,)),
        dma((line * CUT,)), dma((2,)), dma((line * CUT,)), dma((line * CUT,)), dma((line * CUT,)),
        dma((line * CUT,)), dma((line * CUT,)), dma((line * CUT,)),
        dma((2,)), dma((stages,)), dma((stages,)),
    ]
    query_grad, passage_grad, totals = pl.pallas_call(
        functools.partial(kernel, line, groups),
        out_shape=(
            jax.ShapeDtypeStruct(block, bf),
            jax.ShapeDtypeStruct(block, bf),
            jax.ShapeDtypeStruct((8, 128), f32),
        ),
        in_specs=[
            pl.BlockSpec(memory_space=pl.ANY),
            pl.BlockSpec(memory_space=pl.ANY),
            pl.BlockSpec(memory_space=pltpu.SMEM),
            pl.BlockSpec(memory_space=pltpu.SMEM),
        ],
        out_specs=(pl.BlockSpec(memory_space=pltpu.VMEM),) * 3,
        scratch_shapes=scratch,
        compiler_params=pltpu.CompilerParams(
            collective_id=0, has_side_effects=True, vmem_limit_bytes=56 * 1024 * 1024
        ),
    )(queries, passages, block_lists.T, inv_temp.reshape(1))
    pair_count = rows * groups * line * 4
    return query_grad, passage_grad, totals[0, 0] / pair_count, totals[1, 0] / pair_count


def plain(queries, passages, block_lists, inv_temp):
    shard_count = lax.axis_size("shard")
    row_count, feat_width = passages.shape
    listed = block_lists.shape[1]
    col_piece = feat_width // shard_count
    outgoing = passages.reshape(row_count, shard_count, col_piece).transpose(1, 0, 2)
    stripes = lax.all_to_all(outgoing, "shard", split_axis=0, concat_axis=0, tiled=True)
    requests = stripes[block_lists]
    fetched = lax.all_to_all(requests, "shard", split_axis=0, concat_axis=3, tiled=True)
    key_rows = fetched[0]
    logits = inv_temp * jnp.einsum(
        "qd,mkd->mqk", queries, key_rows, preferred_element_type=jnp.float32
    )
    row_peak = jnp.max(logits, axis=(0, 2))
    exp_terms = jnp.exp(logits - row_peak[None, :, None])
    exp_total = jnp.sum(exp_terms, axis=(0, 2))
    row_loss = row_peak + jnp.log(exp_total) - jnp.diagonal(logits[0])
    first_block = (jnp.arange(listed, dtype=jnp.int32) == 0).astype(jnp.float32)
    target = first_block[:, None, None] * jnp.eye(row_count, dtype=jnp.float32)[None]
    residual = exp_terms / exp_total[None, :, None] - target
    weights = residual.astype(jnp.bfloat16)
    temp_part = jnp.sum(residual * logits) / inv_temp
    block_grad = (
        inv_temp * jnp.einsum("mqk,qd->mkd", weights, queries, preferred_element_type=jnp.float32)
    ).astype(jnp.bfloat16)[None]
    query_grad = (
        inv_temp * jnp.einsum("mqk,mkd->qd", weights, key_rows, preferred_element_type=jnp.float32)
    ).astype(jnp.bfloat16)
    block_index = jnp.arange(shard_count, dtype=jnp.int32)
    onehot = (block_lists.reshape(-1)[None, :] == block_index[:, None]).astype(jnp.bfloat16)
    returned = lax.all_to_all(block_grad, "shard", split_axis=3, concat_axis=0, tiled=True)
    summed = jnp.dot(
        onehot,
        returned.reshape(shard_count * listed, row_count * col_piece),
        preferred_element_type=jnp.float32,
    )
    settled = summed.astype(jnp.bfloat16).reshape(shard_count, row_count, col_piece)
    arrived = lax.all_to_all(settled, "shard", split_axis=0, concat_axis=0, tiled=True)
    passage_grad = arrived.transpose(1, 0, 2).reshape(row_count, feat_width)
    totals = lax.psum((jnp.sum(row_loss), temp_part), ("dp", "shard"))
    pair_count = row_count * lax.axis_size("dp") * shard_count
    return query_grad, passage_grad, totals[0] / pair_count, totals[1] / pair_count


def solution(mesh):
    shard_count, groups = mesh.shape["shard"], mesh.shape["dp"]
    line = shard_count // 4
    short = shard_count % 4 == 0 and 2 <= line <= 4 and line & (line - 1) == 0
    body = functools.partial(fused, line, groups) if short and groups & (groups - 1) == 0 else plain
    placed = (P(("dp", "shard"), None), P(("dp", "shard"), None), P("dp", None), P())
    return jax.shard_map(
        body,
        mesh=mesh,
        in_specs=placed,
        out_specs=(P(("dp", "shard"), None), P(("dp", "shard"), None), P(), P()),
        check_vma=False,
    )
```

```python
import functools

import jax
import jax.numpy as jnp
from jax import lax
from jax.experimental import pallas as pl
from jax.experimental.pallas import tpu as pltpu
from jax.sharding import PartitionSpec as P

MESH = pl.DeviceIdType.MESH
LOW = -1e30
NT = (((1,), (1,)), ((), ()))
TN = (((0,), (0,)), ((), ()))
NN = (((1,), (0,)), ((), ()))
CUT = 2
PIECES = 4


def dot(a, b, dims):
    return lax.dot_general(a, b, dims, preferred_element_type=jnp.float32)


def kernel(line, groups, q_in, p_in, lists, temp, qg_out, pg_out, tot_out,
           pcol, qcat, qt, ebuf, wbuf, mrec, stat, stat_in, chip_in, own, zin_r, zin_l,
           zsend, psend, qsend, qrecv, acc, acc_in,
           loc_sem, q_sems, p_recv, p_right, p_left, p_core, st_sems,
           c_send, c_recv, r_send, r_recv, l_send, l_recv, g_sems, a_send, a_recv):
    rows = q_in.shape[0]
    listed = lists.shape[0]
    half = rows // CUT
    wide = 2 * half
    dp = lax.axis_index("dp")
    me = lax.axis_index("shard")
    k = lax.rem(me, 2)
    x = lax.rem(me // 2, 2)
    z = me // 4

    def dev(zz, xx, kk):
        return (dp, (zz * 2 + xx) * 2 + kk)

    core = dev(z, x, 1 - k)
    mate = dev(z, 1 - x, k)
    right = dev(lax.rem(z + 1, line), x, k)
    left = dev(lax.rem(z + line - 1, line), x, k)
    has_r = z < line - 1
    has_l = z > 0
    pairs = [core, mate]
    bit = 1
    far = []
    while bit < line:
        other = z + bit - 2 * bit * lax.rem(z // bit, 2)
        pairs.append(dev(other, x, k))
        if bit > 1:
            far.append(dev(other, x, k))
        bit *= 2
    bit = 1
    while bit < groups:
        other = dp + bit - 2 * bit * lax.rem(dp // bit, 2)
        pairs.append((other, me))
        far.append((other, me))
        bit *= 2

    own_p = [
        pltpu.make_async_copy(
            p_in.at[pl.ds(c * half, half)],
            pcol.at[pl.ds(((z * CUT + c) * 2 + k) * half, half)],
            loc_sem.at[c + 1],
        )
        for c in range(CUT)
    ]
    own_q = pltpu.make_async_copy(q_in, qcat.at[pl.ds(x * rows, rows)], loc_sem.at[0])
    for copy in own_p:
        copy.start()
    own_q.start()

    barrier = pltpu.get_barrier_semaphore()
    for d in [core, mate] + far:
        pl.semaphore_signal(barrier, inc=1, device_id=d, device_id_type=MESH)

    @pl.when(has_r)
    def _():
        pl.semaphore_signal(barrier, inc=1, device_id=right, device_id_type=MESH)

    @pl.when(has_l)
    def _():
        pl.semaphore_signal(barrier, inc=1, device_id=left, device_id_type=MESH)

    ends = jnp.where(has_r, 1, 0) + jnp.where(has_l, 1, 0)
    pl.semaphore_wait(barrier, 2 + len(far) + ends)

    def remote(src, dst, send, recv, d):
        return pltpu.make_async_remote_copy(
            src_ref=src, dst_ref=dst, send_sem=send, recv_sem=recv,
            device_id=d, device_id_type=MESH)

    def p_span(zz, c, kk):
        return pcol.at[pl.ds(((zz * CUT + c) * 2 + kk) * half, half)]

    def p_copy(zz, c, sems, d):
        span = p_span(zz, c, k)
        i = zz * CUT + c
        return remote(span, span, sems.at[i], p_recv.at[i * 2 + k], d)

    def p_wait(zz, c, kk):
        span = p_span(zz, c, kk)
        remote(span, span, p_core.at[0], p_recv.at[(zz * CUT + c) * 2 + kk], core).wait_recv()

    my_rows = pl.ds(x * rows, rows)
    q_copy = remote(qcat.at[my_rows], qcat.at[my_rows], q_sems.at[0], q_sems.at[1], mate)
    mate_rows = pl.ds((1 - x) * rows, rows)
    q_wait = remote(qcat.at[mate_rows], qcat.at[mate_rows], q_sems.at[0], q_sems.at[1], mate)

    for copy in own_p:
        copy.wait()

    for c in range(CUT):
        @pl.when(has_r)
        def _(c=c):
            p_copy(z, c, p_right, right).start()

        @pl.when(has_l)
        def _(c=c):
            p_copy(z, c, p_left, left).start()

    own_q.wait()
    q_copy.start()
    for c in range(CUT):
        p_copy(z, c, p_core, core).start()

    def turn(i):
        qt[:, i * rows:(i + 1) * rows] = qcat[i * rows:(i + 1) * rows, :].T

    @pl.when(x == 0)
    def _():
        turn(0)

    @pl.when(x == 1)
    def _():
        turn(1)

    lane = lax.broadcasted_iota(jnp.int32, (1, 2 * rows), 1)
    jj = lax.broadcasted_iota(jnp.int32, (half, 2 * rows), 0)
    ii = lax.broadcasted_iota(jnp.int32, (half, 2 * rows), 1)
    ahead = jnp.where(ii < rows, ii, ii - rows) - jj
    inv_temp = temp[0]
    row_a = z * 4 + k
    row_b = z * 4 + 2 + k

    def per_lane(block_id, first, last):
        a = jnp.int32(0)
        b = jnp.int32(0)
        for m in range(first, last):
            a = a + jnp.where(lists[m, row_a] == block_id, 1, 0)
            b = b + jnp.where(lists[m, row_b] == block_id, 1, 0)
        return jnp.where(lane < rows, a, b)

    def block_of(zz, kk):
        return zz * 4 + x * 2 + kk

    stat[0:1, :] = jnp.full((1, 2 * rows), LOW, jnp.float32)
    stat[1:8, :] = jnp.zeros((7, 2 * rows), jnp.float32)

    def consume(zz, c):
        part = zz * CUT + c
        live0 = per_lane(block_of(zz, 0), 0, listed) > 0
        live1 = per_lane(block_of(zz, 1), 0, listed) > 0
        pos0 = per_lane(block_of(zz, 0), 0, 1)
        pos1 = per_lane(block_of(zz, 1), 0, 1)
        s = dot(pcol[pl.ds(part * wide, wide)], qt[...], NN) * inv_temp
        s0 = jnp.where(live0, s[:half], LOW)
        s1 = jnp.where(live1, s[half:], LOW)
        s = jnp.concatenate([s0, s1], axis=0)
        m_old = stat[0:1, :]
        m_new = jnp.maximum(m_old, jnp.max(s, axis=0, keepdims=True))
        e = jnp.exp(s - m_new)
        ebuf[part] = e
        scale = jnp.exp(m_old - m_new)
        stat[0:1, :] = m_new
        stat[1:2, :] = stat[1:2, :] * scale + jnp.sum(e, axis=0, keepdims=True)
        stat[2:3, :] = stat[2:3, :] * scale + jnp.sum(e * s, axis=0, keepdims=True)
        diag = jnp.where(ahead == c * half, jnp.where(pos0 > 0, s0, s1), 0.0)
        diag = jnp.sum(diag, axis=0, keepdims=True)
        stat[3:4, :] = stat[3:4, :] + jnp.where(pos0 + pos1 > 0, diag, 0.0)
        mrec[part] = jnp.broadcast_to(m_new, (8, 2 * rows))

    def take_pair(zz, c):
        p_wait(zz, c, 1 - k)
        consume(zz, c)

    q_wait.wait_recv()

    @pl.when(x == 0)
    def _():
        turn(1)

    @pl.when(x == 1)
    def _():
        turn(0)

    @pl.loop(0, (line - 1) * CUT)
    def _(t):
        s = t // CUT
        c = lax.rem(t, CUT)
        from_l = z - 1 - s
        from_r = z + 1 + s

        @pl.when(from_l >= 0)
        def _():
            p_wait(from_l, c, k)

            @pl.when(has_r)
            def _():
                p_copy(from_l, c, p_right, right).start()

            p_copy(from_l, c, p_core, core).start()

        @pl.when(from_r < line)
        def _():
            p_wait(from_r, c, k)

            @pl.when(has_l)
            def _():
                p_copy(from_r, c, p_left, left).start()

            p_copy(from_r, c, p_core, core).start()

        @pl.when(s == 0)
        def _():
            take_pair(z, c)

        @pl.when((s > 0) & (from_l + 1 >= 0) & (from_r - 1 < line))
        def _():
            take_pair(from_r - 1, c)

        @pl.when(from_l >= 0)
        def _():
            take_pair(from_l, c)

        @pl.when((from_r < line) & (from_l < 0))
        def _():
            take_pair(from_r, c)

    st_copy = remote(stat, stat_in, st_sems.at[0], st_sems.at[1], mate)
    st_copy.start()
    st_copy.wait_recv()
    m_loc = stat[0:1, :]
    m_in = stat_in[0:1, :]
    peak = jnp.maximum(m_loc, m_in)
    total = stat[1:2, :] * jnp.exp(m_loc - peak) + stat_in[1:2, :] * jnp.exp(m_in - peak)
    inv_total = 1.0 / total

    own_lane = (lane >= x * rows) & (lane < x * rows + rows)
    diag_row = stat[3:4, :]
    loss = jnp.where(own_lane, peak + jnp.log(total), 0.0) - diag_row
    grad = stat[2:3, :] * (jnp.exp(m_loc - peak) * inv_total) - diag_row
    loss = jnp.sum(loss, axis=1, keepdims=True)
    grad = jnp.sum(grad, axis=1, keepdims=True) / inv_temp
    tile_row = lax.broadcasted_iota(jnp.int32, (8, 128), 0)
    acc[0] = jnp.where(tile_row == 0, loss, grad)
    a_copies = [
        remote(acc.at[i], acc_in.at[i], a_send.at[i], a_recv.at[i], d) for i, d in enumerate(pairs)
    ]
    a_copies[0].start()

    def add_up(i):
        a_copies[i].wait_recv()
        acc[i + 1] = acc[i] + acc_in[i]
        if i + 1 < len(pairs):
            a_copies[i + 1].start()

    def c_copy(d, c):
        i = d * CUT + c
        return remote(psend.at[d, c], chip_in.at[d, c], c_send.at[i], c_recv.at[i], core)

    def r_copy(d, c):
        i = d * CUT + c
        return remote(zsend.at[d, c], zin_r.at[d, c], r_send.at[i], r_recv.at[i], right)

    def l_copy(d, c):
        i = d * CUT + c
        return remote(zsend.at[d, c], zin_l.at[d, c], l_send.at[i], l_recv.at[i], left)

    def give(d):
        pos0 = per_lane(block_of(d, 0), 0, 1) > 0
        pos1 = per_lane(block_of(d, 1), 0, 1) > 0
        for c in range(CUT):
            part = d * CUT + c
            scale = jnp.exp(mrec[part][0:1, :] - peak) * inv_total
            w = ebuf[part] * scale
            w0 = w[:half] - jnp.where(jnp.logical_and(ahead == c * half, pos0), 1.0, 0.0)
            w1 = w[half:] - jnp.where(jnp.logical_and(ahead == c * half, pos1), 1.0, 0.0)
            wbuf[pl.ds(part * wide, half)] = w0.astype(jnp.bfloat16)
            wbuf[pl.ds(part * wide + half, half)] = w1.astype(jnp.bfloat16)
            g = dot(wbuf[pl.ds(part * wide, wide)], qcat[...], NN) * inv_temp
            own[d, pl.ds(2 * c, 2)] = g.reshape(2, half, q_in.shape[1])
            psend[d, c] = own[d, c * 2 + 1 - k].astype(jnp.bfloat16)
            c_copy(d, c).start()

    def take(d, c):
        c_copy(d, c).wait_recv()
        own[d, c * 2 + k] = own[d, c * 2 + k] + chip_in[d, c].astype(jnp.float32)

    for s in range(line - 1):
        dr = line - 1 - s
        dl = s

        @pl.when(dr > z)
        def _(dr=dr):
            give(dr)

        @pl.when(dl < z)
        def _(dl=dl):
            give(dl)

        @pl.when(dr > z)
        def _(s=s, dr=dr):
            for c in range(CUT):
                take(dr, c)

                @pl.when(z == 0)
                def _(c=c):
                    zsend[dr, c] = own[dr, c * 2 + k].astype(jnp.bfloat16)
                    if s == 0:
                        r_copy(dr, c).start()

        @pl.when(dl < z)
        def _(s=s, dl=dl):
            for c in range(CUT):
                take(dl, c)

                @pl.when(z == line - 1)
                def _(c=c):
                    zsend[dl, c] = own[dl, c * 2 + k].astype(jnp.bfloat16)
                    if s == 0:
                        l_copy(dl, c).start()

        if s < 2:
            add_up(s)

    give(z)
    for c in range(CUT):
        take(z, c)

    def q_part(start):
        return dot(wbuf[:, pl.ds(start, rows)], pcol[...], TN) * inv_temp

    def pass_on(t):
        n = t - 1
        ahead_of = n // CUT
        cn = lax.rem(n, CUT)

        @pl.when(z == 0)
        def _():
            r_copy(line - 1 - ahead_of, cn).wait_send()
            r_copy(line - 2 - ahead_of, cn).start()

        @pl.when(z == line - 1)
        def _():
            l_copy(ahead_of, cn).wait_send()
            l_copy(ahead_of + 1, cn).start()

        n = jnp.maximum(t - z, 0)
        dr = line - 1 - n // CUT
        cr = lax.rem(n, CUT)

        @pl.when((t >= z) & (dr > z) & has_l)
        def _():
            r_copy(dr, cr).wait_recv()
            zsend[dr, cr] = (own[dr, cr * 2 + k] + zin_r[dr, cr].astype(jnp.float32)).astype(jnp.bfloat16)
            r_copy(dr, cr).start()

        n = jnp.maximum(t - (line - 1 - z), 0)
        dl = n // CUT
        cl = lax.rem(n, CUT)

        @pl.when((t >= line - 1 - z) & (dl < z) & has_r)
        def _():
            l_copy(dl, cl).wait_recv()
            zsend[dl, cl] = (own[dl, cl * 2 + k] + zin_l[dl, cl].astype(jnp.float32)).astype(jnp.bfloat16)
            l_copy(dl, cl).start()

    last = (line - 2) * CUT
    if last >= 1:
        pass_on(1)

    @pl.when(x == 0)
    def _():
        qsend[...] = q_part(rows).astype(jnp.bfloat16)

    @pl.when(x == 1)
    def _():
        qsend[...] = q_part(0).astype(jnp.bfloat16)

    g_copy = remote(qsend, qrecv, g_sems.at[0], g_sems.at[1], mate)
    g_copy.start()

    add_up(min(2, line - 1))
    if last >= 2:
        pass_on(2)

    @pl.when(x == 0)
    def _():
        qg_out[...] = q_part(0).astype(jnp.bfloat16)

    @pl.when(x == 1)
    def _():
        qg_out[...] = q_part(rows).astype(jnp.bfloat16)

    add_up(min(2, line - 1) + 1)

    @pl.loop(3, last + 1)
    def _(t):
        pass_on(t)

    for i in range(min(2, line - 1) + 2, len(pairs)):
        add_up(i)
    tot_out[...] = acc[len(pairs)]

    g_copy.wait_recv()
    qg_out[...] = (qg_out[...].astype(jnp.float32) + qrecv[...].astype(jnp.float32)).astype(jnp.bfloat16)

    for c in range(CUT):
        @pl.when(has_l)
        def _(c=c):
            r_copy(z, c).wait_recv()
            own[z, c * 2 + k] = own[z, c * 2 + k] + zin_r[z, c].astype(jnp.float32)

        @pl.when(has_r)
        def _(c=c):
            l_copy(z, c).wait_recv()
            own[z, c * 2 + k] = own[z, c * 2 + k] + zin_l[z, c].astype(jnp.float32)

        pg_out[pl.ds(c * half, half)] = own[z, c * 2 + k].astype(jnp.bfloat16)

    q_copy.wait_send()
    st_copy.wait_send()
    g_copy.wait_send()
    for copy in a_copies:
        copy.wait_send()

    @pl.loop(0, line)
    def _(d):
        for c in range(CUT):
            c_copy(d, c).wait_send()
            p_copy(d, c, p_core, core).wait_send()

            @pl.when((d <= z) & has_r)
            def _(c=c):
                p_copy(d, c, p_right, right).wait_send()

            @pl.when((d >= z) & has_l)
            def _(c=c):
                p_copy(d, c, p_left, left).wait_send()

            @pl.when((d > z) & (has_l | (d == 1)))
            def _(c=c):
                r_copy(d, c).wait_send()

            @pl.when((d < z) & (has_r | (d == line - 2)))
            def _(c=c):
                l_copy(d, c).wait_send()


def deliver(pair_count, qg_in, pg_in, totals, qg_out, pg_out, loss, grad, sems):
    part = qg_in.shape[0] // PIECES
    copies = []
    for i in range(PIECES):
        here = pl.ds(i * part, part)
        copies.append(pltpu.make_async_copy(qg_in.at[here], qg_out.at[here], sems.at[0, i]))
        copies.append(pltpu.make_async_copy(pg_in.at[here], pg_out.at[here], sems.at[1, i]))
    for copy in copies:
        copy.start()
    loss[0] = totals[0, 0] / pair_count
    grad[0] = totals[1, 0] / pair_count
    for copy in copies:
        copy.wait()


def fused(line, groups, queries, passages, block_lists, inv_temp):
    rows, width = passages.shape
    stages = 2 + (line.bit_length() - 1) + (groups.bit_length() - 1)
    bf, f32 = jnp.bfloat16, jnp.float32
    block = (rows, width)
    half = rows // CUT
    pieces = (CUT, half, width)
    vm, dma = pltpu.VMEM, pltpu.SemaphoreType.DMA
    scratch = [
        vm((2 * line * rows, width), bf),
        vm((2 * rows, width), bf),
        vm((width, 2 * rows), bf),
        vm((line * CUT, 2 * half, 2 * rows), f32),
        vm((2 * line * rows, 2 * rows), bf),
        vm((line * CUT, 8, 2 * rows), f32),
        vm((8, 2 * rows), f32),
        vm((8, 2 * rows), f32),
        vm((line,) + pieces, bf),
        vm((line, 2 * CUT, half, width), f32),
        vm((line,) + pieces, bf),
        vm((line,) + pieces, bf),
        vm((line,) + pieces, bf),
        vm((line,) + pieces, bf),
        vm(block, bf),
        vm(block, bf),
        vm((stages + 1, 8, 128), f32),
        vm((stages, 8, 128), f32),
        dma((CUT + 1,)), dma((2,)), dma((2 * line * CUT,)), dma((line * CUT,)), dma((line * CUT,)),
        dma((line * CUT,)), dma((2,)), dma((line * CUT,)), dma((line * CUT,)), dma((line * CUT,)),
        dma((line * CUT,)), dma((line * CUT,)), dma((line * CUT,)),
        dma((2,)), dma((stages,)), dma((stages,)),
    ]
    query_grad, passage_grad, totals = pl.pallas_call(
        functools.partial(kernel, line, groups),
        out_shape=(
            jax.ShapeDtypeStruct(block, bf),
            jax.ShapeDtypeStruct(block, bf),
            jax.ShapeDtypeStruct((8, 128), f32),
        ),
        in_specs=[
            pl.BlockSpec(memory_space=pl.ANY),
            pl.BlockSpec(memory_space=pl.ANY),
            pl.BlockSpec(memory_space=pltpu.SMEM),
            pl.BlockSpec(memory_space=pltpu.SMEM),
        ],
        out_specs=(pl.BlockSpec(memory_space=pltpu.VMEM),) * 3,
        scratch_shapes=scratch,
        compiler_params=pltpu.CompilerParams(
            collective_id=0, has_side_effects=True, vmem_limit_bytes=56 * 1024 * 1024
        ),
    )(queries, passages, block_lists.T, inv_temp.reshape(1))
    pair_count = rows * groups * line * 4
    hbm, smem = pl.BlockSpec(memory_space=pltpu.HBM), pl.BlockSpec(memory_space=pltpu.SMEM)
    query_grad, passage_grad, loss_mean, temp_grad = pl.pallas_call(
        functools.partial(deliver, pair_count),
        out_shape=(
            jax.ShapeDtypeStruct(block, bf),
            jax.ShapeDtypeStruct(block, bf),
            jax.ShapeDtypeStruct((1,), f32),
            jax.ShapeDtypeStruct((1,), f32),
        ),
        in_specs=[hbm, hbm, smem],
        out_specs=(hbm, hbm, smem, smem),
        scratch_shapes=[dma((2, PIECES))],
        compiler_params=pltpu.CompilerParams(vmem_limit_bytes=56 * 1024 * 1024),
    )(query_grad, passage_grad, totals)
    return query_grad, passage_grad, loss_mean.reshape(()), temp_grad.reshape(())


def plain(queries, passages, block_lists, inv_temp):
    shard_count = lax.axis_size("shard")
    row_count, feat_width = passages.shape
    listed = block_lists.shape[1]
    col_piece = feat_width // shard_count
    outgoing = passages.reshape(row_count, shard_count, col_piece).transpose(1, 0, 2)
    stripes = lax.all_to_all(outgoing, "shard", split_axis=0, concat_axis=0, tiled=True)
    requests = stripes[block_lists]
    fetched = lax.all_to_all(requests, "shard", split_axis=0, concat_axis=3, tiled=True)
    key_rows = fetched[0]
    logits = inv_temp * jnp.einsum(
        "qd,mkd->mqk", queries, key_rows, preferred_element_type=jnp.float32
    )
    row_peak = jnp.max(logits, axis=(0, 2))
    exp_terms = jnp.exp(logits - row_peak[None, :, None])
    exp_total = jnp.sum(exp_terms, axis=(0, 2))
    row_loss = row_peak + jnp.log(exp_total) - jnp.diagonal(logits[0])
    first_block = (jnp.arange(listed, dtype=jnp.int32) == 0).astype(jnp.float32)
    target = first_block[:, None, None] * jnp.eye(row_count, dtype=jnp.float32)[None]
    residual = exp_terms / exp_total[None, :, None] - target
    weights = residual.astype(jnp.bfloat16)
    temp_part = jnp.sum(residual * logits) / inv_temp
    block_grad = (
        inv_temp * jnp.einsum("mqk,qd->mkd", weights, queries, preferred_element_type=jnp.float32)
    ).astype(jnp.bfloat16)[None]
    query_grad = (
        inv_temp * jnp.einsum("mqk,mkd->qd", weights, key_rows, preferred_element_type=jnp.float32)
    ).astype(jnp.bfloat16)
    block_index = jnp.arange(shard_count, dtype=jnp.int32)
    onehot = (block_lists.reshape(-1)[None, :] == block_index[:, None]).astype(jnp.bfloat16)
    returned = lax.all_to_all(block_grad, "shard", split_axis=3, concat_axis=0, tiled=True)
    summed = jnp.dot(
        onehot,
        returned.reshape(shard_count * listed, row_count * col_piece),
        preferred_element_type=jnp.float32,
    )
    settled = summed.astype(jnp.bfloat16).reshape(shard_count, row_count, col_piece)
    arrived = lax.all_to_all(settled, "shard", split_axis=0, concat_axis=0, tiled=True)
    passage_grad = arrived.transpose(1, 0, 2).reshape(row_count, feat_width)
    totals = lax.psum((jnp.sum(row_loss), temp_part), ("dp", "shard"))
    pair_count = row_count * lax.axis_size("dp") * shard_count
    return query_grad, passage_grad, totals[0] / pair_count, totals[1] / pair_count


def solution(mesh):
    shard_count, groups = mesh.shape["shard"], mesh.shape["dp"]
    line = shard_count // 4
    short = shard_count % 4 == 0 and 2 <= line <= 4 and line & (line - 1) == 0
    body = functools.partial(fused, line, groups) if short and groups & (groups - 1) == 0 else plain
    placed = (P(("dp", "shard"), None), P(("dp", "shard"), None), P("dp", None), P())
    return jax.shard_map(
        body,
        mesh=mesh,
        in_specs=placed,
        out_specs=(P(("dp", "shard"), None), P(("dp", "shard"), None), P(), P()),
        check_vma=False,
    )
```
